512 devices in a mesh: grp: 2 (over x_lo), seq: 32 (over x_hi, z, core), tile: 8 (over y).
Axes of the slice: x: 4 (x_hi: 2, x_lo: 2; x = x_hi * 2 + x_lo), y: 8, z: 8, core: 2. Of those that a mesh axis runs over, the one named last changes fastest.
Arguments:
- enc_features: bfloat16 [8, 80, 64, 512], P('tile', None, 'seq'), may hold values from -6 to 6
- conv_weight: bfloat16 [3, 3, 3, 512, 16], replicated, may hold values from -0.0546875 to 0.0546875
- conv_bias: float32 [16], replicated, may hold values from -0.1 to 0.1
- embed_weight: bfloat16 [64, 4096], replicated, may hold values from -0.75 to 0.75
- embed_bias: float32 [4096], replicated, may hold values from -0.1 to 0.1
- mod_shift: float32 [4096], replicated, may hold values from -0.1 to 0.1
- mod_scale: float32 [4096], replicated, may hold values from -2 to 2
- qkv_weight: bfloat16 [4096, 3, 16, 128], P(None, None, ('grp', 'tile')), may hold values from -0.09375 to 0.09375
- q_gain: float32 [128], replicated, may hold values from 1.5 to 2.5
- k_gain: float32 [128], replicated, may hold values from 1.5 to 2.5
Outputs:
- attended: bfloat16 [32, 16, 20, 2048], P('seq', ('grp', 'tile'))
The draws below stay inside these ranges and needn't reach their ends.
All inputs are finite; a program needn't handle non-finite values.
Results may differ from the reference program's by a relative error of at most 0.015.
Values may be sent and summed in bfloat16 or wider, within the bound.
A program may use at most 64 MiB of HBM per device.

```python
import math
import jax
import jax.numpy as jnp
from jax import lax

D = 4096
HDIM = 128
ZCH = 16
ENC_CH = 512
HEADS = 16
LH = 80
LF = 8
LW = 64
TOKENS = 10240
TOK_DEV = 320
PIECE = 20


def draw_enc_features(key, part):
    key = jax.random.fold_in(key, 11)
    grid_shape = (LF, LH, LW, ENC_CH)
    values = jnp.clip(jax.random.normal(key, grid_shape, jnp.float32), -6.0, 6.0)
    return values.astype(jnp.bfloat16)


def block_scale(stream_key, dims, pieces, smallest, high):
    factor_of = 1.0
    for dim, blocks in pieces:
        draws = jax.random.uniform(jax.random.fold_in(jax.random.fold_in(stream_key, 6), dim), (blocks,), jnp.float32, smallest / len(pieces), high / len(pieces))
        factor_of = factor_of * jnp.repeat(jnp.exp(draws), dims[dim] // blocks).reshape((-1,) + (1,) * (len(dims) - 1 - dim))
    return factor_of


def normal_values(own_key, shape, spread, limit, pieces=(), dtype=jnp.bfloat16):
    loudness = block_scale(own_key, shape, pieces, -0.22, 0.18) if pieces else 1.0
    drawn = jax.random.normal(own_key, shape, jnp.float32) * spread * loudness
    return jnp.minimum(jnp.maximum(drawn, -limit), limit).astype(dtype)


def setup_inputs(seed: int = 0) -> dict:
    arg_keys = jax.random.split(jax.random.key(seed), 11)
    enc_features = draw_enc_features(jax.random.fold_in(arg_keys[10], 71), 0)
    conv_weight = normal_values(arg_keys[1], (3, 3, 3, ENC_CH, ZCH), (27 * ENC_CH) ** -0.5, 0.0546875)
    conv_bias = normal_values(arg_keys[2], (ZCH,), 0.02, 0.1, (), jnp.float32)
    embed_weight = normal_values(arg_keys[3], (4 * ZCH, D), (4 * ZCH) ** -0.5, 0.75)
    embed_bias = normal_values(arg_keys[4], (D,), 0.02, 0.1, (), jnp.float32)
    mod_shift = normal_values(arg_keys[5], (D,), 0.02, 0.1, (), jnp.float32)
    mod_scale = normal_values(arg_keys[6], (D,), 0.3, 2.0, (), jnp.float32)
    qkv_weight = normal_values(arg_keys[7], (D, 3, HEADS, HDIM), D ** -0.5, 0.09375, ((2, 16),))
    q_gain = jnp.clip(jnp.exp(jax.random.uniform(arg_keys[8], (HDIM,), jnp.float32, math.log(1.5), math.log(2.5))), 1.5, 2.5)
    k_gain = jnp.clip(jnp.exp(jax.random.uniform(arg_keys[9], (HDIM,), jnp.float32, math.log(1.5), math.log(2.5))), 1.5, 2.5)
    return {"enc_features": enc_features, "conv_weight": conv_weight, "conv_bias": conv_bias, "embed_weight": embed_weight, "embed_bias": embed_bias, "mod_shift": mod_shift, "mod_scale": mod_scale, "qkv_weight": qkv_weight, "q_gain": q_gain, "k_gain": k_gain}


def conv_latent(enc_features, conv_weight, conv_bias):
    frames, rows, cols, chans = enc_features.shape
    padded = jnp.pad(enc_features, ((1, 1), (1, 1), (1, 1), (0, 0)))
    total = jnp.zeros((frames * rows * cols, conv_weight.shape[4]), jnp.float32)
    for a_tap in range(3):
        for b_tap in range(3):
            for e_tap in range(3):
                window = padded[a_tap:a_tap + frames, b_tap:b_tap + rows, e_tap:e_tap + cols, :]
                total = total + jnp.dot(window.reshape(-1, chans), conv_weight[a_tap, b_tap, e_tap], preferred_element_type=jnp.float32)
    latent = (total + conv_bias).astype(jnp.bfloat16)
    return latent.reshape(frames, rows, cols, -1)

def head_norm(raw, gain):
    scale = lax.rsqrt(lax.optimization_barrier(jnp.mean(raw * raw, axis=-1, keepdims=True)) + 1e-06)
    return (raw * scale * gain).astype(jnp.bfloat16)

def reference(enc_features, conv_weight, conv_bias, embed_weight, embed_bias, mod_shift, mod_scale, qkv_weight, q_gain, k_gain):
    latent = conv_latent(enc_features, conv_weight, conv_bias)
    frames, rows, cols, zch = latent.shape
    patches = latent.reshape(frames, rows // 2, 2, cols // 2, 2, zch)
    patches = patches.transpose(0, 1, 3, 2, 4, 5).reshape(frames * (rows // 2) * (cols // 2), 4 * zch)
    embedded = jnp.dot(patches, embed_weight, preferred_element_type=jnp.float32) + embed_bias
    inv = lax.rsqrt(lax.optimization_barrier(jnp.mean(embedded * embedded, axis=-1, keepdims=True)) + 1e-06)
    normed = (embedded * inv * (1.0 + mod_scale) + mod_shift).astype(jnp.bfloat16)
    width = qkv_weight.shape[0]
    projected = jnp.dot(normed, qkv_weight.reshape(width, -1), preferred_element_type=jnp.float32)
    projected = projected.reshape(-1, 3, HEADS, HDIM)
    queries = head_norm(projected[:, 0], q_gain).transpose(1, 0, 2)
    keys = head_norm(projected[:, 1], k_gain).transpose(1, 0, 2)
    values = projected[:, 2].astype(jnp.bfloat16).transpose(1, 0, 2)
    factor = 1.0 / math.sqrt(HDIM)

    def one_head(triple):
        head_q, head_k, head_v = triple
        scores = jnp.dot(head_q, head_k.T, preferred_element_type=jnp.float32) * factor
        weights = jnp.exp(scores)
        total = lax.optimization_barrier(jnp.sum(weights, axis=1))
        numer = jnp.dot(weights.astype(jnp.bfloat16), head_v, preferred_element_type=jnp.float32)
        return (numer / total[:, None]).astype(jnp.bfloat16)
    heads_out = lax.map(one_head, (queries, keys, values))
    merged = heads_out.transpose(1, 0, 2).reshape(-1, HEADS * HDIM)
    return merged.reshape(TOKENS // TOK_DEV, TOK_DEV // PIECE, PIECE, HEADS * HDIM)
```

```python
import math

import jax
import jax.numpy as jnp
from jax import lax
from jax.experimental import pallas as pl
from jax.experimental.pallas import tpu as pltpu
from jax.sharding import PartitionSpec as P

bf16 = jnp.bfloat16
f32 = jnp.float32

D = 4096
NT = (((1,), (1,)), ((), ()))
EPS = 1e-6


def nt_dot(a, b):
    return lax.dot_general(a, b, NT, preferred_element_type=f32)


def hi_lo(v):
    hi = v.astype(bf16)
    return hi, (v - hi.astype(f32)).astype(bf16)


def conv_block(cw_ref, rho, col):
    zero = jnp.zeros((16, 512), bf16)
    pieces = []
    for a in range(3):
        for ext in range(2):
            for p in range(2):
                for q in range(2):
                    b = rho - p
                    rel = q if ext == 0 else (2 if q == 0 else -1)
                    e = col - rel + 1
                    if 0 <= b <= 2 and 0 <= e <= 2:
                        r = ((a * 3 + b) * 3 + e) * 16
                        pieces.append(cw_ref[r : r + 16, :])
                    else:
                        pieces.append(zero)
    return jnp.concatenate(pieces, axis=0)


def conv_partials(x_ref, cw_ref, g):
    v = x_ref[...].astype(f32).reshape(40, 4, 512)
    part = [v[:, j, :] for j in range(4)]
    edge = jnp.zeros((1, 512), f32)
    acc = None
    for rho in range(4):
        for col in range(2):
            if rho == 0:
                rows = jnp.concatenate([edge, part[2 + col][:39]], axis=0)
            elif rho == 3:
                rows = jnp.concatenate([part[col][1:], edge], axis=0)
            else:
                rows = part[(rho - 1) * 2 + col]
            rows = jnp.where(g == 0, rows[0:24], rows[16:40]).astype(bf16)
            term = nt_dot(rows, conv_block(cw_ref, rho, col))
            acc = term if acc is None else acc + term
    return acc


def kernel(
    x_ref, cw_ref, cbias_ref, emb_hbm, ebias_ref, shift_ref, scale_ref, w_hbm, qg_ref, kg_ref,
    o_ref,
    emb_ref, w_ref, halo_out, halo_in, ybuf, ysend, dens, gat, res, rr, wkv, bias_k, bias_v, gcol,
    kt, vt, qscr, qrows, acc, tot, asend, arecv,
    local_sem, hs_sem, hr_sem, ys_sem, yr_sem, zs_sem, zr_sem, xs_sem, xr_sem, cs_sem, cr_sem, as_sem, ar_sem,
):
    g = lax.axis_index("grp")
    s = lax.axis_index("seq")
    f = lax.axis_index("tile")
    xh, z, core = s // 16, (s // 2) % 8, s % 2
    x = xh * 2 + g
    head = g * 8 + f

    def dev(gg, ss, ff):
        return (gg, ss, ff)

    def x_dev(xx):
        return (xx % 2, (xx // 2) * 16 + z * 2 + core, f)

    def z_dev(zz):
        return (g, xh * 16 + zz * 2 + core, f)

    left, right = lax.rem(s + 31, 32), lax.rem(s + 1, 32)
    before, after = lax.rem(f + 7, 8), lax.rem(f + 1, 8)
    xm, xp, xo = lax.rem(x + 3, 4), lax.rem(x + 1, 4), lax.rem(x + 2, 4)
    partner = (g, s + 1 - 2 * core, f)
    halo_seq = (left, s, right)
    halo_frame = (after, f, before)

    w_copy = pltpu.make_async_copy(w_hbm, w_ref, local_sem.at[0])
    e_copy = pltpu.make_async_copy(emb_hbm, emb_ref, local_sem.at[1])
    e_copy.start()
    w_copy.start()

    barrier = pltpu.get_barrier_semaphore()

    def greet(device):
        pl.semaphore_signal(barrier, inc=1, device_id=device, device_id_type=pl.DeviceIdType.MESH)

    for ss in (left, right):
        for ff in halo_frame:
            greet((g, ss, ff))

    def greet_z(i, _):
        greet(z_dev(lax.rem(z + i, 8)))
        return 0

    lax.fori_loop(1, 8, greet_z, 0)

    def greet_head(i, _):
        j = lax.rem(head + i, 16)
        greet((j // 8, s, j % 8))
        return 0

    lax.fori_loop(1, 16, greet_head, 0)
    greet(x_dev(jnp.where(g == 0, xm, xp)))

    sums = conv_partials(x_ref, cw_ref, g)
    for a in range(3):
        halo_out[a] = sums[:, a * 128 : (a + 1) * 128]
    halo_in[1, 1] = sums[:, 128:256]

    pl.semaphore_wait(barrier, 29)

    def halo_copy(a, t):
        n = a * 3 + t
        return pltpu.make_async_remote_copy(
            src_ref=halo_out.at[a],
            dst_ref=halo_in.at[a, 2 - t],
            send_sem=hs_sem.at[n],
            recv_sem=hr_sem.at[a * 3 + 2 - t],
            device_id=(g, halo_seq[t], halo_frame[a]),
            device_id_type=pl.DeviceIdType.MESH,
        )

    halo = [(a, t) for a in range(3) for t in range(3) if (a, t) != (1, 1)]
    for a, t in halo:
        halo_copy(a, t).start()

    e_copy.wait()
    w_copy.wait()
    res[...] = jnp.zeros_like(res)
    rr[...] = jnp.zeros_like(rr)
    step = 512

    def fold(k, _):
        cols = pl.ds(pl.multiple_of(k * step, step), step)
        e = emb_ref[:, cols]
        gain = 1.0 + scale_ref[:, cols]
        eb = ebias_ref[:, cols]
        e_hi, e_lo = hi_lo(e.astype(f32) * gain)
        rest = jnp.concatenate([eb * gain, shift_ref[:, cols], jnp.zeros((6, step), f32)], axis=0)
        rest_hi, rest_lo = hi_lo(rest)
        rest2 = jnp.concatenate([rest_hi.astype(f32), rest_lo.astype(f32)], axis=0).astype(bf16)
        lhs = jnp.concatenate([e_hi, e_lo, rest2], axis=0)
        w = jnp.concatenate([w_ref[j, cols, :] for j in range(3)], axis=1)
        res[...] += jnp.dot(lhs, w, preferred_element_type=f32)
        b_hi = eb.astype(bf16).astype(f32)
        bias = jnp.concatenate([b_hi, eb - b_hi, jnp.zeros((14, step), f32)], axis=0).astype(bf16)
        both = jnp.concatenate([e, bias, jnp.zeros((48, step), bf16)], axis=0)
        rr[...] += nt_dot(both, both)
        return 0

    lax.fori_loop(0, D // step, fold, 0)

    lane = lax.broadcasted_iota(jnp.int32, (128, 128), 1)
    row = lax.broadcasted_iota(jnp.int32, (128, 128), 0)
    low = lane < 64
    zero64 = jnp.zeros((64, 128), f32)
    for j in range(3):
        cols = slice(j * 128, (j + 1) * 128)
        top = res[0:64, cols] + res[64:128, cols]
        rest = res[128:136, cols] + res[136:144, cols]
        m = jnp.concatenate([top, rest, jnp.zeros((56, 128), f32)], axis=0)
        mt = m.T
        a_t = jnp.where(low, mt, 0.0)
        a_s = pltpu.roll(a_t, 64, 1)
        for half, v in ((0, a_t), (1, a_s)):
            hi, lo = hi_lo(v)
            n = (j * 2 + half) * 128
            wkv[n : n + 128, 0:128] = hi
            wkv[n : n + 128, 128:256] = lo
        if j > 0:
            bias_v_ref = bias_k if j == 1 else bias_v
            bias_v_ref[0] = jnp.broadcast_to(mt[:, 64:65], (128, 128))
            bias_v_ref[1] = jnp.broadcast_to(mt[:, 65:66], (128, 128))
    gram = rr[...]
    g_t = jnp.where(low & (row < 64), gram, 0.0)
    gblock = g_t + pltpu.roll(pltpu.roll(g_t, 64, 1), 64, 0)
    hi, lo = hi_lo(gblock)
    wkv[768:896, 0:128] = hi
    wkv[768:896, 128:256] = lo
    wkv[896:1024, 0:128] = jnp.where(lane == row, 1.0, 0.0).astype(bf16)
    wkv[896:1024, 128:256] = jnp.zeros((128, 128), bf16)
    grow = gram[64:65, :] + gram[65:66, :]
    lane1 = lax.broadcasted_iota(jnp.int32, (1, 128), 1)
    bb = jnp.sum(jnp.where((lane1 == 64) | (lane1 == 65), grow, 0.0), axis=1, keepdims=True)
    grow64 = jnp.where(lane1 < 64, grow, 0.0)
    grow2 = 2.0 * (grow64 + pltpu.roll(grow64, 64, 1))
    gc = gram[:, 64:65] + gram[:, 65:66]
    gc2 = 2.0 * jnp.broadcast_to(jnp.concatenate([gc[0:64], gc[0:64]], axis=0), (128, 128))
    gcol[...] = gc2

    for a, t in halo:
        halo_copy(a, t).wait_recv()
    lane24 = lax.broadcasted_iota(jnp.int32, (24, 128), 1)
    zero24 = jnp.zeros((24, 128), f32)
    has = (f > 0, None, f < 7)
    side = []
    for t in range(3):
        total = None
        for a in range(3):
            v = halo_in[a, t]
            if has[a] is not None:
                v = jnp.where(has[a], v, zero24)
            total = v if total is None else total + v
        side.append(total)
    from_left = jnp.where(s > 0, side[0], zero24)
    from_right = jnp.where(s < 31, side[2], zero24)
    ext = jnp.where((lane24 // 16) % 2 == 0, from_left, from_right)
    lat = side[1] + pltpu.roll(ext, 64, 1)
    cb = jnp.concatenate([cbias_ref[...]] * 8, axis=1)
    lat = (lat + cb).astype(bf16).astype(f32)
    mine = jnp.where(g == 0, lat[0:20], lat[4:24])
    first = mine[0:10]
    second = pltpu.roll(mine[10:20], 64, 1)
    packed = jnp.where(lax.broadcasted_iota(jnp.int32, (10, 128), 1) < 64, first, second)
    packed = jnp.concatenate([packed, jnp.zeros((6, 128), f32)], axis=0).astype(bf16)
    ysend[...] = packed
    ybuf[f] = packed

    def y_copy(i):
        ff = lax.rem(f + i, 8)
        return pltpu.make_async_remote_copy(
            src_ref=ysend, dst_ref=ybuf.at[f], send_sem=ys_sem.at[i], recv_sem=yr_sem.at[i],
            device_id=(g, s, ff), device_id_type=pl.DeviceIdType.MESH,
        )

    for i in range(1, 8):
        y_copy(i).start()

    def y_arrived(i):
        ff = lax.rem(f + 8 - i, 8)
        return pltpu.make_async_remote_copy(
            src_ref=ysend, dst_ref=ybuf.at[ff], send_sem=ys_sem.at[i], recv_sem=yr_sem.at[i],
            device_id=(g, s, ff), device_id_type=pl.DeviceIdType.MESH,
        )

    for i in range(1, 8):
        y_arrived(i).wait_recv()
    for n in range(8):
        dens[n * 10 : n * 10 + 10, :] = ybuf[n, 0:10, :].astype(f32)
    gat[x, core, z] = dens[...].astype(bf16)

    def z_copy(i, zz):
        return pltpu.make_async_remote_copy(
            src_ref=gat.at[x, core, z], dst_ref=gat.at[x, core, z], send_sem=zs_sem.at[i], recv_sem=zr_sem.at[i],
            device_id=z_dev(zz), device_id_type=pl.DeviceIdType.MESH,
        )

    def z_arrived(i, zz):
        return pltpu.make_async_remote_copy(
            src_ref=gat.at[x, core, z], dst_ref=gat.at[x, core, zz], send_sem=zs_sem.at[i], recv_sem=zr_sem.at[i],
            device_id=z_dev(zz), device_id_type=pl.DeviceIdType.MESH,
        )

    for i in (1, 7, 2, 6, 3, 5, 4):
        z_copy(i, lax.rem(z + i, 8)).start()
    for i in (1, 7, 2, 6, 3, 5, 4):
        z_arrived(i, lax.rem(z + 8 - i, 8)).wait_recv()

    def chunk(xx, cc, part):
        ref = gat.at[xx, cc]
        if part == 0:
            return ref
        return ref.at[pl.ds((part - 1) * 4, 4)]

    def x_copy(n, xx, part, to):
        return pltpu.make_async_remote_copy(
            src_ref=chunk(xx, core, part), dst_ref=chunk(xx, core, part), send_sem=xs_sem.at[n],
            recv_sem=xr_sem.at[n], device_id=x_dev(to), device_id_type=pl.DeviceIdType.MESH,
        )

    def c_copy(n, xx, part, cc):
        return pltpu.make_async_remote_copy(
            src_ref=chunk(xx, cc, part), dst_ref=chunk(xx, cc, part), send_sem=cs_sem.at[n],
            recv_sem=cr_sem.at[n], device_id=partner, device_id_type=pl.DeviceIdType.MESH,
        )

    def keys(xx, cc):
        rows = gat[xx, cc].reshape(640, 128)
        p2 = jnp.concatenate([rows, rows], axis=1)
        out = nt_dot(wkv[256:1024, :], p2)
        y = (out[512:640] + jnp.concatenate([gcol[...]] * 5, axis=1)) * out[640:768]
        base = pl.multiple_of((xx * 2 + cc) * 1280, 1280)
        for half in range(2):
            ms = jnp.sum(y[half * 64 : half * 64 + 64], axis=0, keepdims=True) + bb
            inv = lax.rsqrt(jnp.maximum(ms, 0.0) * (1.0 / D) + EPS)
            kr = out[half * 128 : half * 128 + 128]
            kr = (kr + jnp.concatenate([bias_k[0]] * 5, axis=1)) * inv + jnp.concatenate([bias_k[1]] * 5, axis=1)
            ks = lax.rsqrt(jnp.sum(kr * kr, axis=0, keepdims=True) * (1.0 / 128) + EPS)
            cols = pl.ds(base + half * 640, 640)
            kt[:, cols] = (kr * ks).astype(bf16)
            vr = out[256 + half * 128 : 256 + half * 128 + 128]
            vr = (vr + jnp.concatenate([bias_v[0]] * 5, axis=1)) * inv + jnp.concatenate([bias_v[1]] * 5, axis=1)
            vt[:, cols] = vr.astype(bf16)

    other = 1 - core
    x_copy(0, x, 0, xp).start()
    x_copy(1, x, 0, xm).start()
    c_copy(0, x, 0, core).start()
    keys(x, core)
    c_copy(0, x, 0, other).wait_recv()
    keys(x, other)
    x_copy(0, xm, 0, xp).wait_recv()
    x_copy(2, xm, 1, xp).start()
    c_copy(1, xm, 0, core).start()
    x_copy(1, xp, 0, xm).wait_recv()
    x_copy(3, xp, 2, xm).start()
    c_copy(2, xp, 0, core).start()
    keys(xm, core)
    keys(xp, core)
    c_copy(1, xm, 0, other).wait_recv()
    keys(xm, other)
    c_copy(2, xp, 0, other).wait_recv()
    keys(xp, other)
    x_copy(2, xo, 1, xp).wait_recv()
    c_copy(3, xo, 1, core).start()
    x_copy(3, xo, 2, xm).wait_recv()
    c_copy(4, xo, 2, core).start()
    keys(xo, core)
    c_copy(3, xo, 1, other).wait_recv()
    c_copy(4, xo, 2, other).wait_recv()
    keys(xo, other)

    fq, gq, hq = s // 4, (s // 2) % 2, s % 2
    pick_row = lax.broadcasted_iota(jnp.int32, (16, 80), 0)
    pick_col = lax.broadcasted_iota(jnp.int32, (16, 80), 1)
    pick = jnp.where((pick_row < 10) & (pick_col == pick_row + fq * 10), 1.0, 0.0).astype(bf16)
    for hx in range(2):
        blocks = [gat[hx * 2 + gq, cc, zz] for zz in range(8) for cc in range(2)]
        picked = jnp.dot(pick, jnp.concatenate(blocks, axis=1), preferred_element_type=f32)
        for n in range(16):
            qscr[hx * 16 + n] = picked[:, n * 128 : (n + 1) * 128]
    qall = qscr[...]
    for i in range(10):
        qrows[i * 32 : (i + 1) * 32, :] = qall[:, i, :]
    qp = qrows[...]
    qb = qp.astype(bf16)
    q2 = jnp.concatenate([qb, qb], axis=1)
    wq = jnp.where(hq == 0, wkv[0:128, :].astype(f32), wkv[128:256, :].astype(f32)).astype(bf16)
    raw = nt_dot(q2, wq)
    gp = nt_dot(q2, wkv[768:896, :])
    lane320 = lax.broadcasted_iota(jnp.int32, (320, 128), 1)
    y = jnp.where(lane320 // 64 == hq, (gp + grow2) * qp, 0.0)
    ms = jnp.sum(y, axis=1, keepdims=True) + bb
    inv = lax.rsqrt(jnp.maximum(ms, 0.0) * (1.0 / D) + EPS)
    c_q = res[128:129, 0:128] + res[136:137, 0:128]
    d_q = res[129:130, 0:128] + res[137:138, 0:128]
    qr = (raw + c_q) * inv + d_q
    qs = lax.rsqrt(jnp.sum(qr * qr, axis=1, keepdims=True) * (1.0 / 128) + EPS)
    q = (qr * qs * (qg_ref[...] * kg_ref[...] * (math.log2(math.e) / math.sqrt(128.0)))).astype(bf16)

    acc[...] = jnp.zeros_like(acc)
    tot[...] = jnp.zeros_like(tot)
    width = 2560

    def attend(n, _):
        cols = pl.ds(pl.multiple_of(n * width, width), width)
        w = jnp.exp2(jnp.dot(q, kt[:, cols], preferred_element_type=f32))
        t = w[:, 0:128]
        for m in range(1, width // 128):
            t = t + w[:, m * 128 : (m + 1) * 128]
        tot[...] += t
        acc[...] += nt_dot(w.astype(bf16), vt[:, cols])
        return 0

    lax.fori_loop(0, 10240 // width, attend, 0)
    out = acc[...] / jnp.sum(tot[...], axis=1, keepdims=True)
    pad = jnp.zeros((12, 128), f32)
    for j in range(16):
        asend[j] = jnp.concatenate([out[j * 20 : j * 20 + 20], pad], axis=0).astype(bf16)

    def a_copy(i, src, slot, j):
        return pltpu.make_async_remote_copy(
            src_ref=asend.at[src], dst_ref=arecv.at[slot], send_sem=as_sem.at[i], recv_sem=ar_sem.at[i],
            device_id=(j // 8, s, j % 8), device_id_type=pl.DeviceIdType.MESH,
        )

    def send_head(i, _):
        j = lax.rem(head + i, 16)
        a_copy(i, j, head, j).start()
        return 0

    lax.fori_loop(1, 16, send_head, 0)
    arecv[head] = asend[head]

    for a, t in halo:
        halo_copy(a, t).wait_send()
    for i in range(1, 8):
        y_copy(i).wait_send()
        z_copy(i, lax.rem(z + i, 8)).wait_send()
    x_copy(0, x, 0, xp).wait_send()
    x_copy(1, x, 0, xm).wait_send()
    x_copy(2, xm, 1, xp).wait_send()
    x_copy(3, xp, 2, xm).wait_send()
    c_copy(0, x, 0, core).wait_send()
    c_copy(1, xm, 0, core).wait_send()
    c_copy(2, xp, 0, core).wait_send()
    c_copy(3, xo, 1, core).wait_send()
    c_copy(4, xo, 2, core).wait_send()

    def head_arrived(i, _):
        j = lax.rem(head + 16 - i, 16)
        a_copy(i, j, j, j).wait_recv()
        return 0

    lax.fori_loop(1, 16, head_arrived, 0)
    for j in range(16):
        o_ref[:, j * 128 : (j + 1) * 128] = arecv[j, 0:20, :]

    def head_sent(i, _):
        j = lax.rem(head + i, 16)
        a_copy(i, j, head, j).wait_send()
        return 0

    lax.fori_loop(1, 16, head_sent, 0)


def local(
    enc_features, conv_weight, conv_bias, embed_weight, embed_bias, mod_shift, mod_scale, qkv_weight, q_gain, k_gain
):
    vmem = pl.BlockSpec(memory_space=pltpu.VMEM)
    hbm = pl.BlockSpec(memory_space=pl.ANY)
    dma = pltpu.SemaphoreType.DMA
    out = pl.pallas_call(
        kernel,
        out_shape=jax.ShapeDtypeStruct((20, 2048), bf16),
        in_specs=[vmem, vmem, vmem, hbm, vmem, vmem, vmem, hbm, vmem, vmem],
        out_specs=vmem,
        scratch_shapes=[
            pltpu.VMEM((64, D), bf16),
            pltpu.VMEM((3, D, 128), bf16),
            pltpu.VMEM((3, 24, 128), f32),
            pltpu.VMEM((3, 3, 24, 128), f32),
            pltpu.VMEM((8, 16, 128), bf16),
            pltpu.VMEM((16, 128), bf16),
            pltpu.VMEM((80, 128), f32),
            pltpu.VMEM((4, 2, 8, 80, 128), bf16),
            pltpu.VMEM((144, 384), f32),
            pltpu.VMEM((128, 128), f32),
            pltpu.VMEM((1024, 256), bf16),
            pltpu.VMEM((2, 128, 128), f32),
            pltpu.VMEM((2, 128, 128), f32),
            pltpu.VMEM((128, 128), f32),
            pltpu.VMEM((128, 10240), bf16),
            pltpu.VMEM((128, 10240), bf16),
            pltpu.VMEM((32, 16, 128), f32),
            pltpu.VMEM((320, 128), f32),
            pltpu.VMEM((320, 128), f32),
            pltpu.VMEM((320, 128), f32),
            pltpu.VMEM((16, 32, 128), bf16),
            pltpu.VMEM((16, 32, 128), bf16),
            dma((2,)),
            dma((9,)),
            dma((9,)),
            dma((8,)),
            dma((8,)),
            dma((8,)),
            dma((8,)),
            dma((4,)),
            dma((4,)),
            dma((5,)),
            dma((5,)),
            dma((16,)),
            dma((16,)),
        ],
        compiler_params=pltpu.CompilerParams(
            collective_id=0, has_side_effects=True, vmem_limit_bytes=48 * 1024 * 1024
        ),
        cost_estimate=pl.CostEstimate(flops=5_000_000_000, bytes_accessed=6_000_000, transcendentals=3_300_000),
    )(
        enc_features.reshape(80, 2, 512),
        conv_weight.transpose(0, 1, 2, 4, 3).reshape(432, 512),
        conv_bias.reshape(1, 16),
        embed_weight,
        embed_bias.reshape(1, D),
        mod_shift.reshape(1, D),
        mod_scale.reshape(1, D),
        qkv_weight.transpose(1, 2, 0, 3).reshape(3, D, 128),
        q_gain.reshape(1, 128),
        k_gain.reshape(1, 128),
    )
    return out.reshape(1, 1, 20, 2048)


def solution(mesh):
    in_specs = (
        P("tile", None, "seq", None), P(), P(), P(), P(), P(), P(), P(None, None, ("grp", "tile"), None), P(), P(),
    )
    out_specs = P("seq", ("grp", "tile"), None, None)
    return jax.shard_map(local, mesh=mesh, in_specs=in_specs, out_specs=out_specs, check_vma=False)
```

```python
import math

import jax
import jax.numpy as jnp
from jax import lax
from jax.experimental import pallas as pl
from jax.experimental.pallas import tpu as pltpu
from jax.sharding import PartitionSpec as P

bf16 = jnp.bfloat16
f32 = jnp.float32

D = 4096
NT = (((1,), (1,)), ((), ()))
EPS = 1e-6


def nt_dot(a, b):
    return lax.dot_general(a, b, NT, preferred_element_type=f32)


def hi_lo(v):
    hi = v.astype(bf16)
    return hi, (v - hi.astype(f32)).astype(bf16)


def conv_block(cw_ref, rho, col):
    zero = jnp.zeros((16, 512), bf16)
    pieces = []
    for a in range(3):
        for ext in range(2):
            for p in range(2):
                for q in range(2):
                    b = rho - p
                    rel = q if ext == 0 else (2 if q == 0 else -1)
                    e = col - rel + 1
                    if 0 <= b <= 2 and 0 <= e <= 2:
                        r = ((a * 3 + b) * 3 + e) * 16
                        pieces.append(cw_ref[r : r + 16, :])
                    else:
                        pieces.append(zero)
    return jnp.concatenate(pieces, axis=0)


def conv_partials(x_ref, cw_ref, g):
    v = x_ref[...].astype(f32).reshape(40, 4, 512)
    part = [v[:, j, :] for j in range(4)]
    edge = jnp.zeros((1, 512), f32)
    acc = None
    for rho in range(4):
        for col in range(2):
            if rho == 0:
                rows = jnp.concatenate([edge, part[2 + col][:39]], axis=0)
            elif rho == 3:
                rows = jnp.concatenate([part[col][1:], edge], axis=0)
            else:
                rows = part[(rho - 1) * 2 + col]
            rows = jnp.where(g == 0, rows[0:24], rows[16:40]).astype(bf16)
            term = nt_dot(rows, conv_block(cw_ref, rho, col))
            acc = term if acc is None else acc + term
    return acc


def kernel(
    x_hbm, cw_hbm, cbias_hbm, emb_hbm, ebias_hbm, shift_hbm, scale_hbm, w_hbm, qg_hbm, kg_hbm,
    o_ref,
    x_ref, cw_ref, cbias_ref, emb_ref, ebias_ref, shift_ref, scale_ref, w_ref, qg_ref, kg_ref, halo_out, halo_in, ybuf, ysend, dens, gat, res, rr, wkv, bias_k, bias_v, gcol,
    kt, vt, qscr, qrows, acc, tot, asend, arecv,
    local_sem, hs_sem, hr_sem, ys_sem, yr_sem, zs_sem, zr_sem, xs_sem, xr_sem, cs_sem, cr_sem, as_sem, ar_sem,
):
    g = lax.axis_index("grp")
    s = lax.axis_index("seq")
    f = lax.axis_index("tile")
    xh, z, core = s // 16, (s // 2) % 8, s % 2
    x = xh * 2 + g
    head = g * 8 + f

    def dev(gg, ss, ff):
        return (gg, ss, ff)

    def x_dev(xx):
        return (xx % 2, (xx // 2) * 16 + z * 2 + core, f)

    def z_dev(zz):
        return (g, xh * 16 + zz * 2 + core, f)

    left, right = lax.rem(s + 31, 32), lax.rem(s + 1, 32)
    before, after = lax.rem(f + 7, 8), lax.rem(f + 1, 8)
    xm, xp, xo = lax.rem(x + 3, 4), lax.rem(x + 1, 4), lax.rem(x + 2, 4)
    partner = (g, s + 1 - 2 * core, f)
    halo_seq = (left, s, right)
    halo_frame = (after, f, before)

    pairs = (
        (x_hbm, x_ref), (cw_hbm, cw_ref), (cbias_hbm, cbias_ref), (emb_hbm, emb_ref), (ebias_hbm, ebias_ref),
        (shift_hbm, shift_ref), (scale_hbm, scale_ref), (w_hbm, w_ref), (qg_hbm, qg_ref), (kg_hbm, kg_ref),
    )
    fetch = [pltpu.make_async_copy(src, dst, local_sem.at[n]) for n, (src, dst) in enumerate(pairs)]
    for c in fetch:
        c.start()

    barrier = pltpu.get_barrier_semaphore()

    def greet(device):
        pl.semaphore_signal(barrier, inc=1, device_id=device, device_id_type=pl.DeviceIdType.MESH)

    for ss in (left, right):
        for ff in halo_frame:
            greet((g, ss, ff))

    def greet_z(i, _):
        greet(z_dev(lax.rem(z + i, 8)))
        return 0

    lax.fori_loop(1, 8, greet_z, 0)

    def greet_head(i, _):
        j = lax.rem(head + i, 16)
        greet((j // 8, s, j % 8))
        return 0

    lax.fori_loop(1, 16, greet_head, 0)
    greet(x_dev(jnp.where(g == 0, xm, xp)))

    fetch[0].wait()
    fetch[1].wait()
    sums = conv_partials(x_ref, cw_ref, g)
    for a in range(3):
        halo_out[a] = sums[:, a * 128 : (a + 1) * 128]
    halo_in[1, 1] = sums[:, 128:256]

    pl.semaphore_wait(barrier, 29)

    def halo_copy(a, t):
        n = a * 3 + t
        return pltpu.make_async_remote_copy(
            src_ref=halo_out.at[a],
            dst_ref=halo_in.at[a, 2 - t],
            send_sem=hs_sem.at[n],
            recv_sem=hr_sem.at[a * 3 + 2 - t],
            device_id=(g, halo_seq[t], halo_frame[a]),
            device_id_type=pl.DeviceIdType.MESH,
        )

    halo = [(a, t) for a in range(3) for t in range(3) if (a, t) != (1, 1)]
    for a, t in halo:
        halo_copy(a, t).start()

    for c in fetch[2:]:
        c.wait()
    res[...] = jnp.zeros_like(res)
    rr[...] = jnp.zeros_like(rr)
    step = 512

    def fold(k, _):
        cols = pl.ds(pl.multiple_of(k * step, step), step)
        e = emb_ref[:, cols]
        gain = 1.0 + scale_ref[:, cols]
        eb = ebias_ref[:, cols]
        e_hi, e_lo = hi_lo(e.astype(f32) * gain)
        rest = jnp.concatenate([eb * gain, shift_ref[:, cols], jnp.zeros((6, step), f32)], axis=0)
        rest_hi, rest_lo = hi_lo(rest)
        rest2 = jnp.concatenate([rest_hi.astype(f32), rest_lo.astype(f32)], axis=0).astype(bf16)
        lhs = jnp.concatenate([e_hi, e_lo, rest2], axis=0)
        w = jnp.concatenate([w_ref[j, cols, :] for j in range(3)], axis=1)
        res[...] += jnp.dot(lhs, w, preferred_element_type=f32)
        b_hi = eb.astype(bf16).astype(f32)
        bias = jnp.concatenate([b_hi, eb - b_hi, jnp.zeros((14, step), f32)], axis=0).astype(bf16)
        both = jnp.concatenate([e, bias, jnp.zeros((48, step), bf16)], axis=0)
        rr[...] += nt_dot(both, both)
        return 0

    lax.fori_loop(0, D // step, fold, 0)

    lane = lax.broadcasted_iota(jnp.int32, (128, 128), 1)
    row = lax.broadcasted_iota(jnp.int32, (128, 128), 0)
    low = lane < 64
    zero64 = jnp.zeros((64, 128), f32)
    for j in range(3):
        cols = slice(j * 128, (j + 1) * 128)
        top = res[0:64, cols] + res[64:128, cols]
        rest = res[128:136, cols] + res[136:144, cols]
        m = jnp.concatenate([top, rest, jnp.zeros((56, 128), f32)], axis=0)
        mt = m.T
        a_t = jnp.where(low, mt, 0.0)
        a_s = pltpu.roll(a_t, 64, 1)
        for half, v in ((0, a_t), (1, a_s)):
            hi, lo = hi_lo(v)
            n = (j * 2 + half) * 128
            wkv[n : n + 128, 0:128] = hi
            wkv[n : n + 128, 128:256] = lo
        if j > 0:
            bias_v_ref = bias_k if j == 1 else bias_v
            bias_v_ref[0] = jnp.broadcast_to(mt[:, 64:65], (128, 128))
            bias_v_ref[1] = jnp.broadcast_to(mt[:, 65:66], (128, 128))
    gram = rr[...]
    g_t = jnp.where(low & (row < 64), gram, 0.0)
    gblock = g_t + pltpu.roll(pltpu.roll(g_t, 64, 1), 64, 0)
    hi, lo = hi_lo(gblock)
    wkv[768:896, 0:128] = hi
    wkv[768:896, 128:256] = lo
    wkv[896:1024, 0:128] = jnp.where(lane == row, 1.0, 0.0).astype(bf16)
    wkv[896:1024, 128:256] = jnp.zeros((128, 128), bf16)
    grow = gram[64:65, :] + gram[65:66, :]
    lane1 = lax.broadcasted_iota(jnp.int32, (1, 128), 1)
    bb = jnp.sum(jnp.where((lane1 == 64) | (lane1 == 65), grow, 0.0), axis=1, keepdims=True)
    grow64 = jnp.where(lane1 < 64, grow, 0.0)
    grow2 = 2.0 * (grow64 + pltpu.roll(grow64, 64, 1))
    gc = gram[:, 64:65] + gram[:, 65:66]
    gc2 = 2.0 * jnp.broadcast_to(jnp.concatenate([gc[0:64], gc[0:64]], axis=0), (128, 128))
    gcol[...] = gc2

    for a, t in halo:
        halo_copy(a, t).wait_recv()
    lane24 = lax.broadcasted_iota(jnp.int32, (24, 128), 1)
    zero24 = jnp.zeros((24, 128), f32)
    has = (f > 0, None, f < 7)
    side = []
    for t in range(3):
        total = None
        for a in range(3):
            v = halo_in[a, t]
            if has[a] is not None:
                v = jnp.where(has[a], v, zero24)
            total = v if total is None else total + v
        side.append(total)
    from_left = jnp.where(s > 0, side[0], zero24)
    from_right = jnp.where(s < 31, side[2], zero24)
    ext = jnp.where((lane24 // 16) % 2 == 0, from_left, from_right)
    lat = side[1] + pltpu.roll(ext, 64, 1)
    cb = jnp.concatenate([cbias_ref[...]] * 8, axis=1)
    lat = (lat + cb).astype(bf16).astype(f32)
    mine = jnp.where(g == 0, lat[0:20], lat[4:24])
    first = mine[0:10]
    second = pltpu.roll(mine[10:20], 64, 1)
    packed = jnp.where(lax.broadcasted_iota(jnp.int32, (10, 128), 1) < 64, first, second)
    packed = jnp.concatenate([packed, jnp.zeros((6, 128), f32)], axis=0).astype(bf16)
    ysend[...] = packed
    ybuf[f] = packed

    def y_copy(i):
        ff = lax.rem(f + i, 8)
        return pltpu.make_async_remote_copy(
            src_ref=ysend, dst_ref=ybuf.at[f], send_sem=ys_sem.at[i], recv_sem=yr_sem.at[i],
            device_id=(g, s, ff), device_id_type=pl.DeviceIdType.MESH,
        )

    for i in range(1, 8):
        y_copy(i).start()

    def y_arrived(i):
        ff = lax.rem(f + 8 - i, 8)
        return pltpu.make_async_remote_copy(
            src_ref=ysend, dst_ref=ybuf.at[ff], send_sem=ys_sem.at[i], recv_sem=yr_sem.at[i],
            device_id=(g, s, ff), device_id_type=pl.DeviceIdType.MESH,
        )

    for i in range(1, 8):
        y_arrived(i).wait_recv()
    for n in range(8):
        dens[n * 10 : n * 10 + 10, :] = ybuf[n, 0:10, :].astype(f32)
    gat[x, core, z] = dens[...].astype(bf16)

    def z_copy(i, zz):
        return pltpu.make_async_remote_copy(
            src_ref=gat.at[x, core, z], dst_ref=gat.at[x, core, z], send_sem=zs_sem.at[i], recv_sem=zr_sem.at[i],
            device_id=z_dev(zz), device_id_type=pl.DeviceIdType.MESH,
        )

    def z_arrived(i, zz):
        return pltpu.make_async_remote_copy(
            src_ref=gat.at[x, core, z], dst_ref=gat.at[x, core, zz], send_sem=zs_sem.at[i], recv_sem=zr_sem.at[i],
            device_id=z_dev(zz), device_id_type=pl.DeviceIdType.MESH,
        )

    for i in (1, 7, 2, 6, 3, 5, 4):
        z_copy(i, lax.rem(z + i, 8)).start()
    for i in (1, 7, 2, 6, 3, 5, 4):
        z_arrived(i, lax.rem(z + 8 - i, 8)).wait_recv()

    def chunk(xx, cc, part):
        ref = gat.at[xx, cc]
        if part == 0:
            return ref
        return ref.at[pl.ds((part - 1) * 4, 4)]

    def x_copy(n, xx, part, to):
        return pltpu.make_async_remote_copy(
            src_ref=chunk(xx, core, part), dst_ref=chunk(xx, core, part), send_sem=xs_sem.at[n],
            recv_sem=xr_sem.at[n], device_id=x_dev(to), device_id_type=pl.DeviceIdType.MESH,
        )

    def c_copy(n, xx, part, cc):
        return pltpu.make_async_remote_copy(
            src_ref=chunk(xx, cc, part), dst_ref=chunk(xx, cc, part), send_sem=cs_sem.at[n],
            recv_sem=cr_sem.at[n], device_id=partner, device_id_type=pl.DeviceIdType.MESH,
        )

    def keys(xx, cc):
        rows = gat[xx, cc].reshape(640, 128)
        p2 = jnp.concatenate([rows, rows], axis=1)
        out = nt_dot(wkv[256:1024, :], p2)
        y = (out[512:640] + jnp.concatenate([gcol[...]] * 5, axis=1)) * out[640:768]
        base = pl.multiple_of((xx * 2 + cc) * 1280, 1280)
        for half in range(2):
            ms = jnp.sum(y[half * 64 : half * 64 + 64], axis=0, keepdims=True) + bb
            inv = lax.rsqrt(jnp.maximum(ms, 0.0) * (1.0 / D) + EPS)
            kr = out[half * 128 : half * 128 + 128]
            kr = (kr + jnp.concatenate([bias_k[0]] * 5, axis=1)) * inv + jnp.concatenate([bias_k[1]] * 5, axis=1)
            ks = lax.rsqrt(jnp.sum(kr * kr, axis=0, keepdims=True) * (1.0 / 128) + EPS)
            cols = pl.ds(base + half * 640, 640)
            kt[:, cols] = (kr * ks).astype(bf16)
            vr = out[256 + half * 128 : 256 + half * 128 + 128]
            vr = (vr + jnp.concatenate([bias_v[0]] * 5, axis=1)) * inv + jnp.concatenate([bias_v[1]] * 5, axis=1)
            vt[:, cols] = vr.astype(bf16)

    other = 1 - core
    x_copy(0, x, 0, xp).start()
    x_copy(1, x, 0, xm).start()
    c_copy(0, x, 0, core).start()
    keys(x, core)
    c_copy(0, x, 0, other).wait_recv()
    keys(x, other)
    x_copy(0, xm, 0, xp).wait_recv()
    x_copy(2, xm, 1, xp).start()
    c_copy(1, xm, 0, core).start()
    x_copy(1, xp, 0, xm).wait_recv()
    x_copy(3, xp, 2, xm).start()
    c_copy(2, xp, 0, core).start()
    keys(xm, core)
    keys(xp, core)
    c_copy(1, xm, 0, other).wait_recv()
    keys(xm, other)
    c_copy(2, xp, 0, other).wait_recv()
    keys(xp, other)
    x_copy(2, xo, 1, xp).wait_recv()
    c_copy(3, xo, 1, core).start()
    x_copy(3, xo, 2, xm).wait_recv()
    c_copy(4, xo, 2, core).start()
    keys(xo, core)
    c_copy(3, xo, 1, other).wait_recv()
    c_copy(4, xo, 2, other).wait_recv()
    keys(xo, other)

    fq, gq, hq = s // 4, (s // 2) % 2, s % 2
    pick_row = lax.broadcasted_iota(jnp.int32, (16, 80), 0)
    pick_col = lax.broadcasted_iota(jnp.int32, (16, 80), 1)
    pick = jnp.where((pick_row < 10) & (pick_col == pick_row + fq * 10), 1.0, 0.0).astype(bf16)
    for hx in range(2):
        blocks = [gat[hx * 2 + gq, cc, zz] for zz in range(8) for cc in range(2)]
        picked = jnp.dot(pick, jnp.concatenate(blocks, axis=1), preferred_element_type=f32)
        for n in range(16):
            qscr[hx * 16 + n] = picked[:, n * 128 : (n + 1) * 128]
    qall = qscr[...]
    for i in range(10):
        qrows[i * 32 : (i + 1) * 32, :] = qall[:, i, :]
    qp = qrows[...]
    qb = qp.astype(bf16)
    q2 = jnp.concatenate([qb, qb], axis=1)
    wq = jnp.where(hq == 0, wkv[0:128, :].astype(f32), wkv[128:256, :].astype(f32)).astype(bf16)
    raw = nt_dot(q2, wq)
    gp = nt_dot(q2, wkv[768:896, :])
    lane320 = lax.broadcasted_iota(jnp.int32, (320, 128), 1)
    y = jnp.where(lane320 // 64 == hq, (gp + grow2) * qp, 0.0)
    ms = jnp.sum(y, axis=1, keepdims=True) + bb
    inv = lax.rsqrt(jnp.maximum(ms, 0.0) * (1.0 / D) + EPS)
    c_q = res[128:129, 0:128] + res[136:137, 0:128]
    d_q = res[129:130, 0:128] + res[137:138, 0:128]
    qr = (raw + c_q) * inv + d_q
    qs = lax.rsqrt(jnp.sum(qr * qr, axis=1, keepdims=True) * (1.0 / 128) + EPS)
    q = (qr * qs * (qg_ref[...] * kg_ref[...] * (math.log2(math.e) / math.sqrt(128.0)))).astype(bf16)

    acc[...] = jnp.zeros_like(acc)
    tot[...] = jnp.zeros_like(tot)
    width = 2560

    def attend(n, _):
        cols = pl.ds(pl.multiple_of(n * width, width), width)
        w = jnp.exp2(jnp.dot(q, kt[:, cols], preferred_element_type=f32))
        t = w[:, 0:128]
        for m in range(1, width // 128):
            t = t + w[:, m * 128 : (m + 1) * 128]
        tot[...] += t
        acc[...] += nt_dot(w.astype(bf16), vt[:, cols])
        return 0

    lax.fori_loop(0, 10240 // width, attend, 0)
    out = acc[...] / jnp.sum(tot[...], axis=1, keepdims=True)
    pad = jnp.zeros((12, 128), f32)
    for j in range(16):
        asend[j] = jnp.concatenate([out[j * 20 : j * 20 + 20], pad], axis=0).astype(bf16)

    def a_copy(i, src, slot, j):
        return pltpu.make_async_remote_copy(
            src_ref=asend.at[src], dst_ref=arecv.at[slot], send_sem=as_sem.at[i], recv_sem=ar_sem.at[i],
            device_id=(j // 8, s, j % 8), device_id_type=pl.DeviceIdType.MESH,
        )

    def send_head(i, _):
        j = lax.rem(head + i, 16)
        a_copy(i, j, head, j).start()
        return 0

    lax.fori_loop(1, 16, send_head, 0)
    arecv[head] = asend[head]

    for a, t in halo:
        halo_copy(a, t).wait_send()
    for i in range(1, 8):
        y_copy(i).wait_send()
        z_copy(i, lax.rem(z + i, 8)).wait_send()
    x_copy(0, x, 0, xp).wait_send()
    x_copy(1, x, 0, xm).wait_send()
    x_copy(2, xm, 1, xp).wait_send()
    x_copy(3, xp, 2, xm).wait_send()
    c_copy(0, x, 0, core).wait_send()
    c_copy(1, xm, 0, core).wait_send()
    c_copy(2, xp, 0, core).wait_send()
    c_copy(3, xo, 1, core).wait_send()
    c_copy(4, xo, 2, core).wait_send()

    def head_arrived(i, _):
        j = lax.rem(head + 16 - i, 16)
        a_copy(i, j, j, j).wait_recv()
        return 0

    lax.fori_loop(1, 16, head_arrived, 0)
    for j in range(16):
        o_ref[:, j * 128 : (j + 1) * 128] = arecv[j, 0:20, :]

    def head_sent(i, _):
        j = lax.rem(head + i, 16)
        a_copy(i, j, head, j).wait_send()
        return 0

    lax.fori_loop(1, 16, head_sent, 0)


def local(
    enc_features, conv_weight, conv_bias, embed_weight, embed_bias, mod_shift, mod_scale, qkv_weight, q_gain, k_gain
):
    vmem = pl.BlockSpec(memory_space=pltpu.VMEM)
    hbm = pl.BlockSpec(memory_space=pltpu.HBM)
    dma = pltpu.SemaphoreType.DMA
    out = pl.pallas_call(
        kernel,
        out_shape=jax.ShapeDtypeStruct((20, 2048), bf16),
        in_specs=[hbm] * 10,
        out_specs=vmem,
        scratch_shapes=[
            pltpu.VMEM((80, 2, 512), bf16),
            pltpu.VMEM((432, 512), bf16),
            pltpu.VMEM((1, 16), f32),
            pltpu.VMEM((64, D), bf16),
            pltpu.VMEM((1, D), f32),
            pltpu.VMEM((1, D), f32),
            pltpu.VMEM((1, D), f32),
            pltpu.VMEM((3, D, 128), bf16),
            pltpu.VMEM((1, 128), f32),
            pltpu.VMEM((1, 128), f32),
            pltpu.VMEM((3, 24, 128), f32),
            pltpu.VMEM((3, 3, 24, 128), f32),
            pltpu.VMEM((8, 16, 128), bf16),
            pltpu.VMEM((16, 128), bf16),
            pltpu.VMEM((80, 128), f32),
            pltpu.VMEM((4, 2, 8, 80, 128), bf16),
            pltpu.VMEM((144, 384), f32),
            pltpu.VMEM((128, 128), f32),
            pltpu.VMEM((1024, 256), bf16),
            pltpu.VMEM((2, 128, 128), f32),
            pltpu.VMEM((2, 128, 128), f32),
            pltpu.VMEM((128, 128), f32),
            pltpu.VMEM((128, 10240), bf16),
            pltpu.VMEM((128, 10240), bf16),
            pltpu.VMEM((32, 16, 128), f32),
            pltpu.VMEM((320, 128), f32),
            pltpu.VMEM((320, 128), f32),
            pltpu.VMEM((320, 128), f32),
            pltpu.VMEM((16, 32, 128), bf16),
            pltpu.VMEM((16, 32, 128), bf16),
            dma((10,)),
            dma((9,)),
            dma((9,)),
            dma((8,)),
            dma((8,)),
            dma((8,)),
            dma((8,)),
            dma((4,)),
            dma((4,)),
            dma((5,)),
            dma((5,)),
            dma((16,)),
            dma((16,)),
        ],
        compiler_params=pltpu.CompilerParams(
            collective_id=0, has_side_effects=True, vmem_limit_bytes=60 * 1024 * 1024
        ),
        cost_estimate=pl.CostEstimate(flops=5_000_000_000, bytes_accessed=6_000_000, transcendentals=3_300_000),
    )(
        enc_features.reshape(80, 2, 512),
        conv_weight.transpose(0, 1, 2, 4, 3).reshape(432, 512),
        conv_bias.reshape(1, 16),
        embed_weight,
        embed_bias.reshape(1, D),
        mod_shift.reshape(1, D),
        mod_scale.reshape(1, D),
        qkv_weight.transpose(1, 2, 0, 3).reshape(3, D, 128),
        q_gain.reshape(1, 128),
        k_gain.reshape(1, 128),
    )
    return out.reshape(1, 1, 20, 2048)


def solution(mesh):
    in_specs = (
        P("tile", None, "seq", None), P(), P(), P(), P(), P(), P(), P(None, None, ("grp", "tile"), None), P(), P(),
    )
    out_specs = P("seq", ("grp", "tile"), None, None)
    return jax.shard_map(local, mesh=mesh, in_specs=in_specs, out_specs=out_specs, check_vma=False)
```

```python
import math

import jax
import jax.numpy as jnp
from jax import lax
from jax.experimental import pallas as pl
from jax.experimental.pallas import tpu as pltpu
from jax.sharding import PartitionSpec as P

bf16 = jnp.bfloat16
f32 = jnp.float32

D = 4096
NT = (((1,), (1,)), ((), ()))
EPS = 1e-6


def nt_dot(a, b):
    return lax.dot_general(a, b, NT, preferred_element_type=f32)


def hi_lo(v):
    hi = v.astype(bf16)
    return hi, (v - hi.astype(f32)).astype(bf16)


def conv_block(cw_ref, rho, col):
    zero = jnp.zeros((16, 512), bf16)
    pieces = []
    for a in range(3):
        for ext in range(2):
            for p in range(2):
                for q in range(2):
                    b = rho - p
                    rel = q if ext == 0 else (2 if q == 0 else -1)
                    e = col - rel + 1
                    if 0 <= b <= 2 and 0 <= e <= 2:
                        r = ((a * 3 + b) * 3 + e) * 16
                        pieces.append(cw_ref[r : r + 16, :])
                    else:
                        pieces.append(zero)
    return jnp.concatenate(pieces, axis=0)


def conv_partials(x_ref, cw_ref, g):
    v = x_ref[...].astype(f32).reshape(40, 4, 512)
    part = [v[:, j, :] for j in range(4)]
    edge = jnp.zeros((1, 512), f32)
    acc = None
    for rho in range(4):
        for col in range(2):
            if rho == 0:
                rows = jnp.concatenate([edge, part[2 + col][:39]], axis=0)
            elif rho == 3:
                rows = jnp.concatenate([part[col][1:], edge], axis=0)
            else:
                rows = part[(rho - 1) * 2 + col]
            rows = jnp.where(g == 0, rows[0:24], rows[16:40]).astype(bf16)
            term = nt_dot(rows, conv_block(cw_ref, rho, col))
            acc = term if acc is None else acc + term
    return acc


def kernel(
    x_hbm, cw_hbm, cbias_hbm, emb_hbm, ebias_hbm, shift_hbm, scale_hbm, w_hbm, qg_hbm, kg_hbm,
    o_ref,
    x_ref, cw_ref, cbias_ref, emb_ref, ebias_ref, shift_ref, scale_ref, w_ref, qg_ref, kg_ref, halo_out, halo_in, ybuf, ysend, dens, gat, qbuf, res, rr, wkv, wv, bias_k, gcol,
    kt, vt, qrows, acc, asend, arecv,
    local_sem, hs_sem, hr_sem, ys_sem, yr_sem, qs_sem, qr_sem, qc_sem, zs_sem, zr_sem, xs_sem, xr_sem, cs_sem, cr_sem,
    as_sem, ar_sem,
):
    g = lax.axis_index("grp")
    s = lax.axis_index("seq")
    f = lax.axis_index("tile")
    xh, z, core = s // 16, (s // 2) % 8, s % 2
    x = xh * 2 + g
    head = g * 8 + f

    def dev(gg, ss, ff):
        return (gg, ss, ff)

    def x_dev(xx):
        return (xx % 2, (xx // 2) * 16 + z * 2 + core, f)

    def z_dev(zz):
        return (g, xh * 16 + zz * 2 + core, f)

    left, right = lax.rem(s + 31, 32), lax.rem(s + 1, 32)
    before, after = lax.rem(f + 7, 8), lax.rem(f + 1, 8)
    xm, xp, xo = lax.rem(x + 3, 4), lax.rem(x + 1, 4), lax.rem(x + 2, 4)
    partner = (g, s + 1 - 2 * core, f)
    halo_seq = (left, s, right)
    halo_frame = (after, f, before)

    pairs = (
        (x_hbm, x_ref), (cw_hbm, cw_ref), (cbias_hbm, cbias_ref), (emb_hbm, emb_ref), (ebias_hbm, ebias_ref),
        (shift_hbm, shift_ref), (scale_hbm, scale_ref), (w_hbm, w_ref), (qg_hbm, qg_ref), (kg_hbm, kg_ref),
    )
    fetch = [pltpu.make_async_copy(src, dst, local_sem.at[n]) for n, (src, dst) in enumerate(pairs)]
    for c in fetch:
        c.start()

    barrier = pltpu.get_barrier_semaphore()

    def greet(device):
        pl.semaphore_signal(barrier, inc=1, device_id=device, device_id_type=pl.DeviceIdType.MESH)

    for ss in (left, right):
        for ff in halo_frame:
            greet((g, ss, ff))

    def greet_z(i, _):
        greet(z_dev(lax.rem(z + i, 8)))
        return 0

    lax.fori_loop(1, 8, greet_z, 0)

    def greet_head(i, _):
        j = lax.rem(head + i, 16)
        greet((j // 8, s, j % 8))
        return 0

    lax.fori_loop(1, 16, greet_head, 0)
    greet(x_dev(xo))
    greet(x_dev(jnp.where(g == 0, xm, xp)))

    def greet_q(i, _):
        zz = lax.rem(z + i, 8)
        for hx in range(2):
            owner = hx * 2 + z % 2

            @pl.when(owner != x)
            def _():
                greet((owner % 2, hx * 16 + zz * 2 + core, f))

        return 0

    lax.fori_loop(1, 8, greet_q, 0)

    fetch[0].wait()
    fetch[1].wait()
    sums = conv_partials(x_ref, cw_ref, g)
    for a in range(3):
        halo_out[a] = sums[:, a * 128 : (a + 1) * 128]
    halo_in[1, 1] = sums[:, 128:256]

    pl.semaphore_wait(barrier, 30 + jnp.where(z % 2 == g, 9, 12))

    def halo_copy(a, t):
        n = a * 3 + t
        return pltpu.make_async_remote_copy(
            src_ref=halo_out.at[a],
            dst_ref=halo_in.at[a, 2 - t],
            send_sem=hs_sem.at[n],
            recv_sem=hr_sem.at[a * 3 + 2 - t],
            device_id=(g, halo_seq[t], halo_frame[a]),
            device_id_type=pl.DeviceIdType.MESH,
        )

    halo = [(a, t) for a in range(3) for t in range(3) if (a, t) != (1, 1)]
    for a, t in halo:
        halo_copy(a, t).start()

    for c in fetch[2:]:
        c.wait()
    res[...] = jnp.zeros_like(res)
    rr[...] = jnp.zeros_like(rr)
    step = 512

    def fold(k, _):
        cols = pl.ds(pl.multiple_of(k * step, step), step)
        e = emb_ref[:, cols]
        gain = 1.0 + scale_ref[:, cols]
        eb = ebias_ref[:, cols]
        e_hi, e_lo = hi_lo(e.astype(f32) * gain)
        rest = jnp.concatenate([eb * gain, shift_ref[:, cols], jnp.zeros((6, step), f32)], axis=0)
        rest_hi, rest_lo = hi_lo(rest)
        rest2 = jnp.concatenate([rest_hi.astype(f32), rest_lo.astype(f32)], axis=0).astype(bf16)
        lhs = jnp.concatenate([e_hi, e_lo, rest2], axis=0)
        w = jnp.concatenate([w_ref[j, cols, :] for j in range(3)], axis=1)
        res[...] += jnp.dot(lhs, w, preferred_element_type=f32)
        b_hi = eb.astype(bf16).astype(f32)
        bias = jnp.concatenate([b_hi, eb - b_hi, jnp.zeros((14, step), f32)], axis=0).astype(bf16)
        both = jnp.concatenate([e, bias, jnp.zeros((48, step), bf16)], axis=0)
        rr[...] += nt_dot(both, both)
        return 0

    lax.fori_loop(0, D // step, fold, 0)

    lane = lax.broadcasted_iota(jnp.int32, (128, 128), 1)
    row = lax.broadcasted_iota(jnp.int32, (128, 128), 0)
    low = lane < 64
    for j in range(3):
        cols = slice(j * 128, (j + 1) * 128)
        top = res[0:64, cols] + res[64:128, cols]
        rest = res[128:136, cols] + res[136:144, cols]
        if j == 2:
            row8 = lax.broadcasted_iota(jnp.int32, (8, 128), 0)
            rest = jnp.where(row8 == 2, rest[0:1, :], rest)
            m = jnp.concatenate([top, rest, jnp.zeros((56, 128), f32)], axis=0)
            hi, lo = hi_lo(m)
            wv[0:128] = hi
            wv[128:256] = hi
            wv[256:384] = lo
            continue
        m = jnp.concatenate([top, rest, jnp.zeros((56, 128), f32)], axis=0)
        mt = m.T
        a_t = jnp.where(low, mt, 0.0)
        a_s = pltpu.roll(a_t, 64, 1)
        for half, v in ((0, a_t), (1, a_s)):
            hi, lo = hi_lo(v)
            n = (j * 2 + half) * 128
            wkv[n : n + 128, 0:128] = hi
            wkv[n : n + 128, 128:256] = lo
        if j == 1:
            bias_k[0] = jnp.broadcast_to(mt[:, 64:65], (128, 128))
            bias_k[1] = jnp.broadcast_to(mt[:, 65:66], (128, 128))
    gram = rr[...]
    g_t = jnp.where(low & (row < 64), gram, 0.0)
    gblock = g_t + pltpu.roll(pltpu.roll(g_t, 64, 1), 64, 0)
    hi, lo = hi_lo(gblock)
    wkv[512:640, 0:128] = hi
    wkv[512:640, 128:256] = lo
    wkv[640:768, 0:128] = jnp.where(lane == row, 1.0, 0.0).astype(bf16)
    wkv[640:768, 128:256] = jnp.zeros((128, 128), bf16)
    grow = gram[64:65, :] + gram[65:66, :]
    lane1 = lax.broadcasted_iota(jnp.int32, (1, 128), 1)
    bb = jnp.sum(jnp.where((lane1 == 64) | (lane1 == 65), grow, 0.0), axis=1, keepdims=True)
    grow64 = jnp.where(lane1 < 64, grow, 0.0)
    grow2 = 2.0 * (grow64 + pltpu.roll(grow64, 64, 1))
    gc = gram[:, 64:65] + gram[:, 65:66]
    gc2 = 2.0 * jnp.broadcast_to(jnp.concatenate([gc[0:64], gc[0:64]], axis=0), (128, 128))
    gcol[...] = gc2
    vt[64:128, :] = jnp.zeros((64, 10240), bf16)
    acc[...] = jnp.zeros_like(acc)

    for a, t in halo:
        halo_copy(a, t).wait_recv()
    lane24 = lax.broadcasted_iota(jnp.int32, (24, 128), 1)
    zero24 = jnp.zeros((24, 128), f32)
    has = (f > 0, None, f < 7)
    side = []
    for t in range(3):
        total = None
        for a in range(3):
            v = halo_in[a, t]
            if has[a] is not None:
                v = jnp.where(has[a], v, zero24)
            total = v if total is None else total + v
        side.append(total)
    from_left = jnp.where(s > 0, side[0], zero24)
    from_right = jnp.where(s < 31, side[2], zero24)
    ext = jnp.where((lane24 // 16) % 2 == 0, from_left, from_right)
    lat = side[1] + pltpu.roll(ext, 64, 1)
    cb = jnp.concatenate([cbias_ref[...]] * 8, axis=1)
    lat = (lat + cb).astype(bf16).astype(f32)
    mine = jnp.where(g == 0, lat[0:20], lat[4:24])
    first = mine[0:10]
    second = pltpu.roll(mine[10:20], 64, 1)
    packed = jnp.where(lax.broadcasted_iota(jnp.int32, (10, 128), 1) < 64, first, second)
    packed = jnp.concatenate([packed, jnp.zeros((6, 128), f32)], axis=0).astype(bf16)
    ysend[...] = packed
    ybuf[f] = packed

    def y_copy(i):
        ff = lax.rem(f + i, 8)
        return pltpu.make_async_remote_copy(
            src_ref=ysend, dst_ref=ybuf.at[f], send_sem=ys_sem.at[i], recv_sem=yr_sem.at[i],
            device_id=(g, s, ff), device_id_type=pl.DeviceIdType.MESH,
        )

    for i in range(1, 8):
        y_copy(i).start()

    def y_arrived(i):
        ff = lax.rem(f + 8 - i, 8)
        return pltpu.make_async_remote_copy(
            src_ref=ysend, dst_ref=ybuf.at[ff], send_sem=ys_sem.at[i], recv_sem=yr_sem.at[i],
            device_id=(g, s, ff), device_id_type=pl.DeviceIdType.MESH,
        )

    for i in range(1, 8):
        y_arrived(i).wait_recv()
    for n in range(8):
        dens[n * 10 : n * 10 + 10, :] = ybuf[n, 0:10, :].astype(f32)
    gat[z, x, core] = dens[...].astype(bf16)

    def q_copy(xq, k):
        zq = 2 * k + g
        return pltpu.make_async_remote_copy(
            src_ref=ybuf.at[4 * (xq // 2) + k], dst_ref=qbuf.at[core, xh * 8 + z], send_sem=qs_sem.at[xq * 4 + k],
            recv_sem=qr_sem.at[xh * 8 + z], device_id=(xq % 2, (xq // 2) * 16 + zq * 2 + core, f),
            device_id_type=pl.DeviceIdType.MESH,
        )

    def q_away(xq, k):
        return (x != xq) | (z != 2 * k + g)

    for xq in range(4):
        for k in range(4):

            @pl.when(q_away(xq, k))
            def _():
                q_copy(xq, k).start()

    @pl.when(z % 2 == g)
    def _():
        pltpu.make_async_copy(
            ybuf.at[4 * xh + z // 2], qbuf.at[core, xh * 8 + z], qr_sem.at[xh * 8 + z]
        ).start()

    steps = (0, 1, 7, 2, 6, 3, 5, 4)

    def at(n):
        return lax.rem(z + steps[n], 8)

    def z_copy(i, zz):
        return pltpu.make_async_remote_copy(
            src_ref=gat.at[z, x, core], dst_ref=gat.at[z, x, core], send_sem=zs_sem.at[i], recv_sem=zr_sem.at[i],
            device_id=z_dev(zz), device_id_type=pl.DeviceIdType.MESH,
        )

    def z_arrived(n):
        i = 8 - steps[n]
        return pltpu.make_async_remote_copy(
            src_ref=gat.at[z, x, core], dst_ref=gat.at[at(n), x, core], send_sem=zs_sem.at[i], recv_sem=zr_sem.at[i],
            device_id=z_dev(at(n)), device_id_type=pl.DeviceIdType.MESH,
        )

    def x_copy(n, d):
        piece = gat.at[at(n), x, core]
        return pltpu.make_async_remote_copy(
            src_ref=piece, dst_ref=piece, send_sem=xs_sem.at[n, d], recv_sem=xr_sem.at[at(n), d],
            device_id=x_dev(lax.rem(x + d, 4)), device_id_type=pl.DeviceIdType.MESH,
        )

    def x_arrived(n, d):
        xx = lax.rem(x + 4 - d, 4)
        piece = gat.at[at(n), xx, core]
        return pltpu.make_async_remote_copy(
            src_ref=piece, dst_ref=piece, send_sem=xs_sem.at[n, d], recv_sem=xr_sem.at[at(n), d],
            device_id=x_dev(xx), device_id_type=pl.DeviceIdType.MESH,
        )

    def c_copy(n, d, cc):
        xx = lax.rem(x + d, 4)
        piece = gat.at[at(n), xx, cc]
        return pltpu.make_async_remote_copy(
            src_ref=piece, dst_ref=piece, send_sem=cs_sem.at[n, d], recv_sem=cr_sem.at[n, d],
            device_id=partner, device_id_type=pl.DeviceIdType.MESH,
        )

    def spread(n):
        if n > 0:
            z_arrived(n).wait_recv()
        for d in (2, 1, 3):
            x_copy(n, d).start()
        c_copy(n, 0, core).start()

    def share(n):
        for d in (1, 3, 2):
            x_arrived(n, d).wait_recv()
            c_copy(n, 4 - d, core).start()

    def complete(n):
        for d in range(4):
            c_copy(n, d, 1 - core).wait_recv()

    def keys(m):
        rows = jnp.concatenate([gat[at(n)].reshape(640, 128) for n in (2 * m, 2 * m + 1)], axis=0)
        p2 = jnp.concatenate([rows, rows], axis=1)
        out = nt_dot(wkv[256:768, :], p2)
        pt = out[384:512]
        y = (out[256:384] + jnp.concatenate([gcol[...]] * 10, axis=1)) * pt
        row8 = lax.broadcasted_iota(jnp.int32, (16, 1280), 0)
        for half in range(2):
            ms = jnp.sum(y[half * 64 : half * 64 + 64], axis=0, keepdims=True) + bb
            inv = lax.rsqrt(jnp.maximum(ms, 0.0) * (1.0 / D) + EPS)
            kr = out[half * 128 : half * 128 + 128]
            kr = (kr + jnp.concatenate([bias_k[0]] * 10, axis=1)) * inv + jnp.concatenate([bias_k[1]] * 10, axis=1)
            ks = lax.rsqrt(jnp.sum(kr * kr, axis=0, keepdims=True) * (1.0 / 128) + EPS)
            cols = slice(m * 2560 + half * 1280, m * 2560 + half * 1280 + 1280)
            kt[:, cols] = (kr * ks).astype(bf16)
            vt[0:64, cols] = (pt[half * 64 : half * 64 + 64] * inv).astype(bf16)
            inv_hi = inv.astype(bf16).astype(f32)
            extra = jnp.where(row8 == 0, inv_hi, jnp.where(row8 == 1, 1.0, jnp.where(row8 == 2, inv - inv_hi, 0.0)))
            vt[64:80, cols] = extra.astype(bf16)

    def attend(m):
        cols = slice(m * 2560, m * 2560 + 2560)
        w = jnp.exp2(jnp.dot(q, kt[:, cols], preferred_element_type=f32))
        acc[...] += nt_dot(w.astype(bf16), vt[:, cols])

    for i in (1, 7, 2, 6, 3, 5, 4):
        z_copy(i, lax.rem(z + i, 8)).start()
    spread(0)
    spread(1)
    spread(2)
    share(0)
    spread(3)
    spread(4)
    for n in range(16):
        pltpu.make_async_copy(ybuf.at[0], qbuf.at[core, n], qr_sem.at[n]).wait()

    def q_share(cc):
        return pltpu.make_async_remote_copy(
            src_ref=qbuf.at[cc], dst_ref=qbuf.at[cc], send_sem=qc_sem.at[0], recv_sem=qc_sem.at[1],
            device_id=partner, device_id_type=pl.DeviceIdType.MESH,
        )

    q_share(core).start()
    spread(5)
    spread(6)
    spread(7)
    share(1)
    complete(0)
    complete(1)
    keys(0)
    q_share(1 - core).wait_recv()
    hq = core
    for cc in range(2):
        qall = qbuf[cc].astype(f32)
        for i in range(10):
            qrows[pl.ds(i * 32 + cc, 16, stride=2), :] = qall[:, i, :]
    qp = qrows[...]
    qb = qp.astype(bf16)
    q2 = jnp.concatenate([qb, qb], axis=1)
    wq = jnp.where(hq == 0, wkv[0:128, :].astype(f32), wkv[128:256, :].astype(f32)).astype(bf16)
    raw = nt_dot(q2, wq)
    gp = nt_dot(q2, wkv[512:640, :])
    lane320 = lax.broadcasted_iota(jnp.int32, (320, 128), 1)
    y = jnp.where(lane320 // 64 == hq, (gp + grow2) * qp, 0.0)
    ms = jnp.sum(y, axis=1, keepdims=True) + bb
    inv = lax.rsqrt(jnp.maximum(ms, 0.0) * (1.0 / D) + EPS)
    c_q = res[128:129, 0:128] + res[136:137, 0:128]
    d_q = res[129:130, 0:128] + res[137:138, 0:128]
    qr = (raw + c_q) * inv + d_q
    qs = lax.rsqrt(jnp.sum(qr * qr, axis=1, keepdims=True) * (1.0 / 128) + EPS)
    q = (qr * qs * (qg_ref[...] * kg_ref[...] * (math.log2(math.e) / math.sqrt(128.0)))).astype(bf16)
    share(2)
    share(3)
    attend(0)
    share(4)
    share(5)
    complete(2)
    complete(3)
    keys(1)
    attend(1)
    share(6)
    share(7)
    complete(4)
    complete(5)
    keys(2)
    attend(2)
    complete(6)
    complete(7)
    keys(3)
    attend(3)
    u = acc[...]
    hi, lo = hi_lo(u)
    numer = jnp.dot(jnp.concatenate([hi, lo, hi], axis=1), wv[...], preferred_element_type=f32)
    out = numer / u[:, 65:66]
    pad = jnp.zeros((12, 128), f32)
    for j in range(16):
        asend[j] = jnp.concatenate([out[j * 20 : j * 20 + 20], pad], axis=0).astype(bf16)

    def a_copy(i, src, slot, j):
        return pltpu.make_async_remote_copy(
            src_ref=asend.at[src], dst_ref=arecv.at[slot], send_sem=as_sem.at[i], recv_sem=ar_sem.at[i],
            device_id=(j // 8, s, j % 8), device_id_type=pl.DeviceIdType.MESH,
        )

    def send_head(i, _):
        j = lax.rem(head + i, 16)
        a_copy(i, j, head, j).start()
        return 0

    lax.fori_loop(1, 16, send_head, 0)
    arecv[head] = asend[head]

    for a, t in halo:
        halo_copy(a, t).wait_send()
    for i in range(1, 8):
        y_copy(i).wait_send()
        z_copy(i, lax.rem(z + i, 8)).wait_send()
    for xq in range(4):
        for k in range(4):

            @pl.when(q_away(xq, k))
            def _():
                q_copy(xq, k).wait_send()

    q_share(core).wait_send()
    for n in range(8):
        for d in range(1, 4):
            x_copy(n, d).wait_send()
        for d in range(4):
            c_copy(n, d, core).wait_send()

    def head_arrived(i, _):
        j = lax.rem(head + 16 - i, 16)
        a_copy(i, j, j, j).wait_recv()
        return 0

    lax.fori_loop(1, 16, head_arrived, 0)
    for j in range(16):
        o_ref[:, j * 128 : (j + 1) * 128] = arecv[j, 0:20, :]

    def head_sent(i, _):
        j = lax.rem(head + i, 16)
        a_copy(i, j, head, j).wait_send()
        return 0

    lax.fori_loop(1, 16, head_sent, 0)


def local(
    enc_features, conv_weight, conv_bias, embed_weight, embed_bias, mod_shift, mod_scale, qkv_weight, q_gain, k_gain
):
    vmem = pl.BlockSpec(memory_space=pltpu.VMEM)
    hbm = pl.BlockSpec(memory_space=pltpu.HBM)
    dma = pltpu.SemaphoreType.DMA
    out = pl.pallas_call(
        kernel,
        out_shape=jax.ShapeDtypeStruct((20, 2048), bf16),
        in_specs=[hbm] * 10,
        out_specs=vmem,
        scratch_shapes=[
            pltpu.VMEM((80, 2, 512), bf16),
            pltpu.VMEM((432, 512), bf16),
            pltpu.VMEM((1, 16), f32),
            pltpu.VMEM((64, D), bf16),
            pltpu.VMEM((1, D), f32),
            pltpu.VMEM((1, D), f32),
            pltpu.VMEM((1, D), f32),
            pltpu.VMEM((3, D, 128), bf16),
            pltpu.VMEM((1, 128), f32),
            pltpu.VMEM((1, 128), f32),
            pltpu.VMEM((3, 24, 128), f32),
            pltpu.VMEM((3, 3, 24, 128), f32),
            pltpu.VMEM((8, 16, 128), bf16),
            pltpu.VMEM((16, 128), bf16),
            pltpu.VMEM((80, 128), f32),
            pltpu.VMEM((8, 4, 2, 80, 128), bf16),
            pltpu.VMEM((2, 16, 16, 128), bf16),
            pltpu.VMEM((144, 384), f32),
            pltpu.VMEM((128, 128), f32),
            pltpu.VMEM((768, 256), bf16),
            pltpu.VMEM((384, 128), bf16),
            pltpu.VMEM((2, 128, 128), f32),
            pltpu.VMEM((128, 128), f32),
            pltpu.VMEM((128, 10240), bf16),
            pltpu.VMEM((128, 10240), bf16),
            pltpu.VMEM((320, 128), f32),
            pltpu.VMEM((320, 128), f32),
            pltpu.VMEM((16, 32, 128), bf16),
            pltpu.VMEM((16, 32, 128), bf16),
            dma((10,)),
            dma((9,)),
            dma((9,)),
            dma((8,)),
            dma((8,)),
            dma((16,)),
            dma((16,)),
            dma((2,)),
            dma((8,)),
            dma((8,)),
            dma((8, 4)),
            dma((8, 4)),
            dma((8, 4)),
            dma((8, 4)),
            dma((16,)),
            dma((16,)),
        ],
        compiler_params=pltpu.CompilerParams(
            collective_id=0, has_side_effects=True, vmem_limit_bytes=60 * 1024 * 1024
        ),
        cost_estimate=pl.CostEstimate(flops=5_000_000_000, bytes_accessed=6_000_000, transcendentals=3_300_000),
    )(
        enc_features.reshape(80, 2, 512),
        conv_weight.transpose(0, 1, 2, 4, 3).reshape(432, 512),
        conv_bias.reshape(1, 16),
        embed_weight,
        embed_bias.reshape(1, D),
        mod_shift.reshape(1, D),
        mod_scale.reshape(1, D),
        qkv_weight.transpose(1, 2, 0, 3).reshape(3, D, 128),
        q_gain.reshape(1, 128),
        k_gain.reshape(1, 128),
    )
    return out.reshape(1, 1, 20, 2048)


def solution(mesh):
    in_specs = (
        P("tile", None, "seq", None), P(), P(), P(), P(), P(), P(), P(None, None, ("grp", "tile"), None), P(), P(),
    )
    out_specs = P("seq", ("grp", "tile"), None, None)
    return jax.shard_map(local, mesh=mesh, in_specs=in_specs, out_specs=out_specs, check_vma=False)
```

```python
import math

import jax
import jax.numpy as jnp
from jax import lax
from jax.experimental import pallas as pl
from jax.experimental.pallas import tpu as pltpu
from jax.sharding import PartitionSpec as P

bf16 = jnp.bfloat16
f32 = jnp.float32

D = 4096
NT = (((1,), (1,)), ((), ()))
EPS = 1e-6


def nt_dot(a, b):
    return lax.dot_general(a, b, NT, preferred_element_type=f32)


def hi_lo(v):
    hi = v.astype(bf16)
    return hi, (v - hi.astype(f32)).astype(bf16)


def conv_block(cw_ref, rho, col):
    zero = jnp.zeros((16, 512), bf16)
    pieces = []
    for a in range(3):
        for ext in range(2):
            for p in range(2):
                for q in range(2):
                    b = rho - p
                    rel = q if ext == 0 else (2 if q == 0 else -1)
                    e = col - rel + 1
                    if 0 <= b <= 2 and 0 <= e <= 2:
                        r = ((a * 3 + b) * 3 + e) * 16
                        pieces.append(cw_ref[r : r + 16, :])
                    else:
                        pieces.append(zero)
    return jnp.concatenate(pieces, axis=0)


def conv_partials(x_ref, cw_ref, g):
    v = x_ref[...].astype(f32).reshape(40, 4, 512)
    part = [v[:, j, :] for j in range(4)]
    edge = jnp.zeros((1, 512), f32)
    acc = None
    for rho in range(4):
        for col in range(2):
            if rho == 0:
                rows = jnp.concatenate([edge, part[2 + col][:39]], axis=0)
            elif rho == 3:
                rows = jnp.concatenate([part[col][1:], edge], axis=0)
            else:
                rows = part[(rho - 1) * 2 + col]
            rows = jnp.where(g == 0, rows[0:24], rows[16:40]).astype(bf16)
            term = nt_dot(rows, conv_block(cw_ref, rho, col))
            acc = term if acc is None else acc + term
    return acc


def kernel(
    x_hbm, cw_hbm, cbias_hbm, emb_hbm, ebias_hbm, shift_hbm, scale_hbm, w_hbm, qg_hbm, kg_hbm,
    o_ref,
    x_ref, cw_ref, cbias_ref, emb_ref, ebias_ref, shift_ref, scale_ref, w_ref, qg_ref, kg_ref, halo_out, halo_in, ybuf, ysend, dens, gat, res, rr, wkv, wv, bias_k, gcol,
    kt, vt, qscr, qrows, acc, asend, arecv,
    local_sem, hs_sem, hr_sem, ys_sem, yr_sem, zs_sem, zr_sem, xs_sem, xr_sem, cs_sem, cr_sem,
    as_sem, ar_sem,
):
    g = lax.axis_index("grp")
    s = lax.axis_index("seq")
    f = lax.axis_index("tile")
    xh, z, core = s // 16, (s // 2) % 8, s % 2
    x = xh * 2 + g
    head = g * 8 + f

    def dev(gg, ss, ff):
        return (gg, ss, ff)

    def x_dev(xx):
        return (xx % 2, (xx // 2) * 16 + z * 2 + core, f)

    def z_dev(zz):
        return (g, xh * 16 + zz * 2 + core, f)

    left, right = lax.rem(s + 31, 32), lax.rem(s + 1, 32)
    before, after = lax.rem(f + 7, 8), lax.rem(f + 1, 8)
    xm, xp, xo = lax.rem(x + 3, 4), lax.rem(x + 1, 4), lax.rem(x + 2, 4)
    partner = (g, s + 1 - 2 * core, f)
    halo_seq = (left, s, right)
    halo_frame = (after, f, before)

    pairs = (
        (x_hbm, x_ref), (cw_hbm, cw_ref), (cbias_hbm, cbias_ref), (emb_hbm, emb_ref), (ebias_hbm, ebias_ref),
        (shift_hbm, shift_ref), (scale_hbm, scale_ref), (w_hbm, w_ref), (qg_hbm, qg_ref), (kg_hbm, kg_ref),
    )
    fetch = [pltpu.make_async_copy(src, dst, local_sem.at[n]) for n, (src, dst) in enumerate(pairs)]
    fetch[0].start()
    fetch[1].start()

    barrier = pltpu.get_barrier_semaphore()

    def greet(device):
        pl.semaphore_signal(barrier, inc=1, device_id=device, device_id_type=pl.DeviceIdType.MESH)

    for ss in (left, right):
        for ff in halo_frame:
            greet((g, ss, ff))

    def greet_z(i, _):
        greet(z_dev(lax.rem(z + i, 8)))
        return 0

    lax.fori_loop(1, 8, greet_z, 0)

    def greet_head(i, _):
        j = lax.rem(head + i, 16)
        greet((j // 8, s, j % 8))
        return 0

    lax.fori_loop(1, 16, greet_head, 0)
    greet(x_dev(xo))
    greet(x_dev(jnp.where(g == 0, xm, xp)))

    for c in fetch[2:]:
        c.start()
    fetch[0].wait()
    fetch[1].wait()
    sums = conv_partials(x_ref, cw_ref, g)
    for a in range(3):
        halo_out[a] = sums[:, a * 128 : (a + 1) * 128]
    halo_in[1, 1] = sums[:, 128:256]

    pl.semaphore_wait(barrier, 30)

    def halo_copy(a, t):
        n = a * 3 + t
        return pltpu.make_async_remote_copy(
            src_ref=halo_out.at[a],
            dst_ref=halo_in.at[a, 2 - t],
            send_sem=hs_sem.at[n],
            recv_sem=hr_sem.at[a * 3 + 2 - t],
            device_id=(g, halo_seq[t], halo_frame[a]),
            device_id_type=pl.DeviceIdType.MESH,
        )

    halo = [(a, t) for a in range(3) for t in range(3) if (a, t) != (1, 1)]
    for a, t in halo:
        halo_copy(a, t).start()

    for c in fetch[2:]:
        c.wait()
    res[...] = jnp.zeros_like(res)
    rr[...] = jnp.zeros_like(rr)
    step = 512

    def fold(k, _):
        cols = pl.ds(pl.multiple_of(k * step, step), step)
        e = emb_ref[:, cols]
        gain = 1.0 + scale_ref[:, cols]
        eb = ebias_ref[:, cols]
        e_hi, e_lo = hi_lo(e.astype(f32) * gain)
        rest = jnp.concatenate([eb * gain, shift_ref[:, cols], jnp.zeros((6, step), f32)], axis=0)
        rest_hi, rest_lo = hi_lo(rest)
        rest2 = jnp.concatenate([rest_hi.astype(f32), rest_lo.astype(f32)], axis=0).astype(bf16)
        lhs = jnp.concatenate([e_hi, e_lo, rest2], axis=0)
        w = jnp.concatenate([w_ref[j, cols, :] for j in range(3)], axis=1)
        res[...] += jnp.dot(lhs, w, preferred_element_type=f32)
        b_hi = eb.astype(bf16).astype(f32)
        bias = jnp.concatenate([b_hi, eb - b_hi, jnp.zeros((14, step), f32)], axis=0).astype(bf16)
        both = jnp.concatenate([e, bias, jnp.zeros((48, step), bf16)], axis=0)
        rr[...] += nt_dot(both, both)
        return 0

    lax.fori_loop(0, D // step, fold, 0)

    lane = lax.broadcasted_iota(jnp.int32, (128, 128), 1)
    row = lax.broadcasted_iota(jnp.int32, (128, 128), 0)
    low = lane < 64
    for j in range(3):
        cols = slice(j * 128, (j + 1) * 128)
        top = res[0:64, cols] + res[64:128, cols]
        rest = res[128:136, cols] + res[136:144, cols]
        if j == 2:
            row8 = lax.broadcasted_iota(jnp.int32, (8, 128), 0)
            rest = jnp.where(row8 == 2, rest[0:1, :], rest)
            m = jnp.concatenate([top, rest, jnp.zeros((56, 128), f32)], axis=0)
            hi, lo = hi_lo(m)
            wv[0:128] = hi
            wv[128:256] = hi
            wv[256:384] = lo
            continue
        m = jnp.concatenate([top, rest, jnp.zeros((56, 128), f32)], axis=0)
        mt = m.T
        a_t = jnp.where(low, mt, 0.0)
        a_s = pltpu.roll(a_t, 64, 1)
        for half, v in ((0, a_t), (1, a_s)):
            hi, lo = hi_lo(v)
            n = (j * 2 + half) * 128
            wkv[n : n + 128, 0:128] = hi
            wkv[n : n + 128, 128:256] = lo
        if j == 1:
            bias_k[0] = jnp.broadcast_to(mt[:, 64:65], (128, 128))
            bias_k[1] = jnp.broadcast_to(mt[:, 65:66], (128, 128))
    gram = rr[...]
    g_t = jnp.where(low & (row < 64), gram, 0.0)
    gblock = g_t + pltpu.roll(pltpu.roll(g_t, 64, 1), 64, 0)
    hi, lo = hi_lo(gblock)
    wkv[512:640, 0:128] = hi
    wkv[512:640, 128:256] = lo
    wkv[640:768, 0:128] = jnp.where(lane == row, 1.0, 0.0).astype(bf16)
    wkv[640:768, 128:256] = jnp.zeros((128, 128), bf16)
    grow = gram[64:65, :] + gram[65:66, :]
    lane1 = lax.broadcasted_iota(jnp.int32, (1, 128), 1)
    bb = jnp.sum(jnp.where((lane1 == 64) | (lane1 == 65), grow, 0.0), axis=1, keepdims=True)
    grow64 = jnp.where(lane1 < 64, grow, 0.0)
    grow2 = 2.0 * (grow64 + pltpu.roll(grow64, 64, 1))
    gc = gram[:, 64:65] + gram[:, 65:66]
    gc2 = 2.0 * jnp.broadcast_to(jnp.concatenate([gc[0:64], gc[0:64]], axis=0), (128, 128))
    gcol[...] = gc2
    vt[64:128, :] = jnp.zeros((64, 10240), bf16)
    acc[...] = jnp.zeros_like(acc)

    for a, t in halo:
        halo_copy(a, t).wait_recv()
    lane24 = lax.broadcasted_iota(jnp.int32, (24, 128), 1)
    zero24 = jnp.zeros((24, 128), f32)
    has = (f > 0, None, f < 7)
    side = []
    for t in range(3):
        total = None
        for a in range(3):
            v = halo_in[a, t]
            if has[a] is not None:
                v = jnp.where(has[a], v, zero24)
            total = v if total is None else total + v
        side.append(total)
    from_left = jnp.where(s > 0, side[0], zero24)
    from_right = jnp.where(s < 31, side[2], zero24)
    ext = jnp.where((lane24 // 16) % 2 == 0, from_left, from_right)
    lat = side[1] + pltpu.roll(ext, 64, 1)
    cb = jnp.concatenate([cbias_ref[...]] * 8, axis=1)
    lat = (lat + cb).astype(bf16).astype(f32)
    mine = jnp.where(g == 0, lat[0:20], lat[4:24])
    first = mine[0:10]
    second = pltpu.roll(mine[10:20], 64, 1)
    packed = jnp.where(lax.broadcasted_iota(jnp.int32, (10, 128), 1) < 64, first, second)
    packed = jnp.concatenate([packed, jnp.zeros((6, 128), f32)], axis=0).astype(bf16)
    ysend[...] = packed
    ybuf[f] = packed

    def y_copy(i):
        ff = lax.rem(f + i, 8)
        return pltpu.make_async_remote_copy(
            src_ref=ysend, dst_ref=ybuf.at[f], send_sem=ys_sem.at[i], recv_sem=yr_sem.at[i],
            device_id=(g, s, ff), device_id_type=pl.DeviceIdType.MESH,
        )

    for i in range(1, 8):
        y_copy(i).start()

    def y_arrived(i):
        ff = lax.rem(f + 8 - i, 8)
        return pltpu.make_async_remote_copy(
            src_ref=ysend, dst_ref=ybuf.at[ff], send_sem=ys_sem.at[i], recv_sem=yr_sem.at[i],
            device_id=(g, s, ff), device_id_type=pl.DeviceIdType.MESH,
        )

    for i in range(1, 8):
        y_arrived(i).wait_recv()
    for n in range(8):
        dens[n * 10 : n * 10 + 10, :] = ybuf[n, 0:10, :].astype(f32)
    gat[z, x, core] = dens[...].astype(bf16)

    def at(n):
        if n == 0:
            return z
        return jnp.where(z > n - 1, n - 1, n)

    def z_copy(i, zz):
        return pltpu.make_async_remote_copy(
            src_ref=gat.at[z, x, core], dst_ref=gat.at[z, x, core], send_sem=zs_sem.at[i], recv_sem=zr_sem.at[i],
            device_id=z_dev(zz), device_id_type=pl.DeviceIdType.MESH,
        )

    def z_arrived(n):
        i = lax.rem(z + 8 - at(n), 8)
        return pltpu.make_async_remote_copy(
            src_ref=gat.at[z, x, core], dst_ref=gat.at[at(n), x, core], send_sem=zs_sem.at[i], recv_sem=zr_sem.at[i],
            device_id=z_dev(at(n)), device_id_type=pl.DeviceIdType.MESH,
        )

    def x_copy(n, d):
        piece = gat.at[at(n), x, core]
        return pltpu.make_async_remote_copy(
            src_ref=piece, dst_ref=piece, send_sem=xs_sem.at[n, d], recv_sem=xr_sem.at[at(n), d],
            device_id=x_dev(lax.rem(x + d, 4)), device_id_type=pl.DeviceIdType.MESH,
        )

    def x_arrived(n, d):
        xx = lax.rem(x + 4 - d, 4)
        piece = gat.at[at(n), xx, core]
        return pltpu.make_async_remote_copy(
            src_ref=piece, dst_ref=piece, send_sem=xs_sem.at[n, d], recv_sem=xr_sem.at[at(n), d],
            device_id=x_dev(xx), device_id_type=pl.DeviceIdType.MESH,
        )

    def c_copy(n, d, cc):
        xx = lax.rem(x + d, 4)
        piece = gat.at[at(n), xx, cc]
        return pltpu.make_async_remote_copy(
            src_ref=piece, dst_ref=piece, send_sem=cs_sem.at[n, d], recv_sem=cr_sem.at[n, d],
            device_id=partner, device_id_type=pl.DeviceIdType.MESH,
        )

    def spread(n):
        if n > 0:
            z_arrived(n).wait_recv()
        for d in (2, 1, 3):
            x_copy(n, d).start()
        c_copy(n, 0, core).start()

    def share(n):
        for d in (1, 3, 2):
            x_arrived(n, d).wait_recv()
            c_copy(n, 4 - d, core).start()

    def complete(n):
        for d in range(4):
            c_copy(n, d, 1 - core).wait_recv()

    def keys(*pieces):
        rows = jnp.concatenate([gat[at(n)].reshape(640, 128) for n in pieces], axis=0)
        size = 640 * len(pieces)
        wide = size // 128
        p2 = jnp.concatenate([rows, rows], axis=1)
        out = nt_dot(wkv[256:768, :], p2)
        pt = out[384:512]
        y = (out[256:384] + jnp.concatenate([gcol[...]] * wide, axis=1)) * pt
        row16 = lax.broadcasted_iota(jnp.int32, (16, size), 0)
        for half in range(2):
            ms = jnp.sum(y[half * 64 : half * 64 + 64], axis=0, keepdims=True) + bb
            inv = lax.rsqrt(jnp.maximum(ms, 0.0) * (1.0 / D) + EPS)
            kr = out[half * 128 : half * 128 + 128]
            kr = (kr + jnp.concatenate([bias_k[0]] * wide, axis=1)) * inv + jnp.concatenate([bias_k[1]] * wide, axis=1)
            ks = lax.rsqrt(jnp.sum(kr * kr, axis=0, keepdims=True) * (1.0 / 128) + EPS)
            first = pieces[0] * 1280 + half * size
            cols = slice(first, first + size)
            kt[:, cols] = (kr * ks).astype(bf16)
            vt[0:64, cols] = (pt[half * 64 : half * 64 + 64] * inv).astype(bf16)
            inv_hi = inv.astype(bf16).astype(f32)
            extra = jnp.where(row16 == 0, inv_hi, jnp.where(row16 == 1, 1.0, jnp.where(row16 == 2, inv - inv_hi, 0.0)))
            vt[64:80, cols] = extra.astype(bf16)

    def attend(*pieces):
        cols = slice(pieces[0] * 1280, pieces[-1] * 1280 + 1280)
        w = jnp.exp2(jnp.dot(q, kt[:, cols], preferred_element_type=f32))
        acc[...] += nt_dot(w.astype(bf16), vt[:, cols])

    for i in (1, 7, 2, 6, 3, 5, 4):
        z_copy(i, lax.rem(z + i, 8)).start()
    spread(0)
    for n in range(1, 8):
        spread(n)
    share(0)
    share(1)
    share(2)
    complete(0)
    keys(0)
    share(3)
    complete(1)
    keys(1)
    share(4)
    complete(2)
    keys(2)
    share(5)
    complete(3)
    keys(3)
    share(6)
    complete(4)
    keys(4)
    share(7)
    complete(5)
    complete(6)
    keys(5, 6)
    complete(7)
    fq, gq, hq = s // 4, z % 2, core
    pick_row = lax.broadcasted_iota(jnp.int32, (16, 80), 0)
    pick_col = lax.broadcasted_iota(jnp.int32, (16, 80), 1)
    pick = jnp.where((pick_row < 10) & (pick_col == pick_row + fq * 10), 1.0, 0.0).astype(bf16)
    for hx in range(2):
        blocks = [gat[zz, hx * 2 + gq, cc] for zz in range(8) for cc in range(2)]
        picked = jnp.dot(pick, jnp.concatenate(blocks, axis=1), preferred_element_type=f32)
        for n in range(16):
            qscr[hx * 16 + n] = picked[:, n * 128 : (n + 1) * 128]
    qall = qscr[...]
    for i in range(10):
        qrows[i * 32 : (i + 1) * 32, :] = qall[:, i, :]
    qp = qrows[...]
    qb = qp.astype(bf16)
    q2 = jnp.concatenate([qb, qb], axis=1)
    wq = jnp.where(hq == 0, wkv[0:128, :].astype(f32), wkv[128:256, :].astype(f32)).astype(bf16)
    raw = nt_dot(q2, wq)
    gp = nt_dot(q2, wkv[512:640, :])
    lane320 = lax.broadcasted_iota(jnp.int32, (320, 128), 1)
    y = jnp.where(lane320 // 64 == hq, (gp + grow2) * qp, 0.0)
    ms = jnp.sum(y, axis=1, keepdims=True) + bb
    inv = lax.rsqrt(jnp.maximum(ms, 0.0) * (1.0 / D) + EPS)
    c_q = res[128:129, 0:128] + res[136:137, 0:128]
    d_q = res[129:130, 0:128] + res[137:138, 0:128]
    qr = (raw + c_q) * inv + d_q
    qs = lax.rsqrt(jnp.sum(qr * qr, axis=1, keepdims=True) * (1.0 / 128) + EPS)
    q = (qr * qs * (qg_ref[...] * kg_ref[...] * (math.log2(math.e) / math.sqrt(128.0)))).astype(bf16)
    attend(0, 1)
    attend(2, 3)
    keys(7)
    attend(4, 5)
    attend(6, 7)
    u = acc[...]
    hi, lo = hi_lo(u)
    numer = jnp.dot(jnp.concatenate([hi, lo, hi], axis=1), wv[...], preferred_element_type=f32)
    out = numer / u[:, 65:66]
    pad = jnp.zeros((12, 128), f32)
    for j in range(16):
        asend[j] = jnp.concatenate([out[j * 20 : j * 20 + 20], pad], axis=0).astype(bf16)

    def a_copy(i, src, slot, j):
        return pltpu.make_async_remote_copy(
            src_ref=asend.at[src], dst_ref=arecv.at[slot], send_sem=as_sem.at[i], recv_sem=ar_sem.at[i],
            device_id=(j // 8, s, j % 8), device_id_type=pl.DeviceIdType.MESH,
        )

    def send_head(i, _):
        j = lax.rem(head + i, 16)
        a_copy(i, j, head, j).start()
        return 0

    lax.fori_loop(1, 16, send_head, 0)
    arecv[head] = asend[head]

    for a, t in halo:
        halo_copy(a, t).wait_send()
    for i in range(1, 8):
        y_copy(i).wait_send()
        z_copy(i, lax.rem(z + i, 8)).wait_send()
    for n in range(8):
        for d in range(1, 4):
            x_copy(n, d).wait_send()
        for d in range(4):
            c_copy(n, d, core).wait_send()

    def head_arrived(i, _):
        j = lax.rem(head + 16 - i, 16)
        a_copy(i, j, j, j).wait_recv()
        return 0

    lax.fori_loop(1, 16, head_arrived, 0)
    for j in range(16):
        o_ref[:, j * 128 : (j + 1) * 128] = arecv[j, 0:20, :]

    def head_sent(i, _):
        j = lax.rem(head + i, 16)
        a_copy(i, j, head, j).wait_send()
        return 0

    lax.fori_loop(1, 16, head_sent, 0)


def local(
    enc_features, conv_weight, conv_bias, embed_weight, embed_bias, mod_shift, mod_scale, qkv_weight, q_gain, k_gain
):
    vmem = pl.BlockSpec(memory_space=pltpu.VMEM)
    hbm = pl.BlockSpec(memory_space=pltpu.HBM)
    dma = pltpu.SemaphoreType.DMA
    out = pl.pallas_call(
        kernel,
        out_shape=jax.ShapeDtypeStruct((20, 2048), bf16),
        in_specs=[hbm] * 10,
        out_specs=vmem,
        scratch_shapes=[
            pltpu.VMEM((80, 2, 512), bf16),
            pltpu.VMEM((432, 512), bf16),
            pltpu.VMEM((1, 16), f32),
            pltpu.VMEM((64, D), bf16),
            pltpu.VMEM((1, D), f32),
            pltpu.VMEM((1, D), f32),
            pltpu.VMEM((1, D), f32),
            pltpu.VMEM((3, D, 128), bf16),
            pltpu.VMEM((1, 128), f32),
            pltpu.VMEM((1, 128), f32),
            pltpu.VMEM((3, 24, 128), f32),
            pltpu.VMEM((3, 3, 24, 128), f32),
            pltpu.VMEM((8, 16, 128), bf16),
            pltpu.VMEM((16, 128), bf16),
            pltpu.VMEM((80, 128), f32),
            pltpu.VMEM((8, 4, 2, 80, 128), bf16),
            pltpu.VMEM((144, 384), f32),
            pltpu.VMEM((128, 128), f32),
            pltpu.VMEM((768, 256), bf16),
            pltpu.VMEM((384, 128), bf16),
            pltpu.VMEM((2, 128, 128), f32),
            pltpu.VMEM((128, 128), f32),
            pltpu.VMEM((128, 10240), bf16),
            pltpu.VMEM((128, 10240), bf16),
            pltpu.VMEM((32, 16, 128), f32),
            pltpu.VMEM((320, 128), f32),
            pltpu.VMEM((320, 128), f32),
            pltpu.VMEM((16, 32, 128), bf16),
            pltpu.VMEM((16, 32, 128), bf16),
            dma((10,)),
            dma((9,)),
            dma((9,)),
            dma((8,)),
            dma((8,)),
            dma((8,)),
            dma((8,)),
            dma((8, 4)),
            dma((8, 4)),
            dma((8, 4)),
            dma((8, 4)),
            dma((16,)),
            dma((16,)),
        ],
        compiler_params=pltpu.CompilerParams(
            collective_id=0, has_side_effects=True, vmem_limit_bytes=60 * 1024 * 1024
        ),
        cost_estimate=pl.CostEstimate(flops=5_000_000_000, bytes_accessed=6_000_000, transcendentals=3_300_000),
    )(
        enc_features.reshape(80, 2, 512),
        conv_weight.transpose(0, 1, 2, 4, 3).reshape(432, 512),
        conv_bias.reshape(1, 16),
        embed_weight,
        embed_bias.reshape(1, D),
        mod_shift.reshape(1, D),
        mod_scale.reshape(1, D),
        qkv_weight.transpose(1, 2, 0, 3).reshape(3, D, 128),
        q_gain.reshape(1, 128),
        k_gain.reshape(1, 128),
    )
    return out.reshape(1, 1, 20, 2048)


def solution(mesh):
    in_specs = (
        P("tile", None, "seq", None), P(), P(), P(), P(), P(), P(), P(None, None, ("grp", "tile"), None), P(), P(),
    )
    out_specs = P("seq", ("grp", "tile"), None, None)
    return jax.shard_map(local, mesh=mesh, in_specs=in_specs, out_specs=out_specs, check_vma=False)
```

```python
import math

import jax
import jax.numpy as jnp
from jax import lax
from jax.experimental import pallas as pl
from jax.experimental.pallas import tpu as pltpu
from jax.sharding import PartitionSpec as P

bf16 = jnp.bfloat16
f32 = jnp.float32

D = 4096
NT = (((1,), (1,)), ((), ()))
EPS = 1e-6


def nt_dot(a, b):
    return lax.dot_general(a, b, NT, preferred_element_type=f32)


def hi_lo(v):
    hi = v.astype(bf16)
    return hi, (v - hi.astype(f32)).astype(bf16)


def conv_block(cw_ref, rho, col):
    zero = jnp.zeros((16, 512), bf16)
    pieces = []
    for a in range(3):
        for ext in range(2):
            for p in range(2):
                for q in range(2):
                    b = rho - p
                    rel = q if ext == 0 else (2 if q == 0 else -1)
                    e = col - rel + 1
                    if 0 <= b <= 2 and 0 <= e <= 2:
                        r = ((a * 3 + b) * 3 + e) * 16
                        pieces.append(cw_ref[r : r + 16, :])
                    else:
                        pieces.append(zero)
    return jnp.concatenate(pieces, axis=0)


def conv_partials(x_ref, cw_ref, g):
    v = x_ref[...].astype(f32).reshape(40, 4, 512)
    part = [v[:, j, :] for j in range(4)]
    edge = jnp.zeros((1, 512), f32)
    acc = None
    for rho in range(4):
        for col in range(2):
            if rho == 0:
                rows = jnp.concatenate([edge, part[2 + col][:39]], axis=0)
            elif rho == 3:
                rows = jnp.concatenate([part[col][1:], edge], axis=0)
            else:
                rows = part[(rho - 1) * 2 + col]
            rows = jnp.where(g == 0, rows[0:24], rows[16:40]).astype(bf16)
            term = nt_dot(rows, conv_block(cw_ref, rho, col))
            acc = term if acc is None else acc + term
    return acc


def kernel(
    x_hbm, cw_hbm, cbias_hbm, emb_hbm, ebias_hbm, shift_hbm, scale_hbm, w_hbm, qg_hbm, kg_hbm,
    arecv,
    x_ref, cw_ref, cbias_ref, emb_ref, ebias_ref, shift_ref, scale_ref, w_ref, qg_ref, kg_ref, halo_out, halo_in, ybuf, ysend, dens, gat, res, rr, wkv, wv, bias_k, gcol,
    kt, vt, qscr, qrows, acc, asend,
    local_sem, hs_sem, hr_sem, ys_sem, yr_sem, zs_sem, zr_sem, xs_sem, xr_sem, cs_sem, cr_sem,
    as_sem, ar_sem,
):
    g = lax.axis_index("grp")
    s = lax.axis_index("seq")
    f = lax.axis_index("tile")
    xh, z, core = s // 16, (s // 2) % 8, s % 2
    x = xh * 2 + g
    head = g * 8 + f

    def dev(gg, ss, ff):
        return (gg, ss, ff)

    def x_dev(xx):
        return (xx % 2, (xx // 2) * 16 + z * 2 + core, f)

    def z_dev(zz):
        return (g, xh * 16 + zz * 2 + core, f)

    left, right = lax.rem(s + 31, 32), lax.rem(s + 1, 32)
    before, after = lax.rem(f + 7, 8), lax.rem(f + 1, 8)
    xm, xp, xo = lax.rem(x + 3, 4), lax.rem(x + 1, 4), lax.rem(x + 2, 4)
    partner = (g, s + 1 - 2 * core, f)
    halo_seq = (left, s, right)
    halo_frame = (after, f, before)

    pairs = (
        (x_hbm, x_ref), (cw_hbm, cw_ref), (cbias_hbm, cbias_ref), (emb_hbm, emb_ref), (ebias_hbm, ebias_ref),
        (shift_hbm, shift_ref), (scale_hbm, scale_ref), (w_hbm, w_ref), (qg_hbm, qg_ref), (kg_hbm, kg_ref),
    )
    fetch = [pltpu.make_async_copy(src, dst, local_sem.at[n]) for n, (src, dst) in enumerate(pairs)]
    fetch[0].start()
    fetch[1].start()

    barrier = pltpu.get_barrier_semaphore()

    def greet(device):
        pl.semaphore_signal(barrier, inc=1, device_id=device, device_id_type=pl.DeviceIdType.MESH)

    for ss in (left, right):
        for ff in halo_frame:
            greet((g, ss, ff))

    def greet_z(i, _):
        greet(z_dev(lax.rem(z + i, 8)))
        return 0

    lax.fori_loop(1, 8, greet_z, 0)

    def greet_head(i, _):
        j = lax.rem(head + i, 16)
        greet((j // 8, s, j % 8))
        return 0

    lax.fori_loop(1, 16, greet_head, 0)
    greet(x_dev(xo))
    greet(x_dev(jnp.where(g == 0, xm, xp)))

    for c in fetch[2:]:
        c.start()
    fetch[0].wait()
    fetch[1].wait()
    sums = conv_partials(x_ref, cw_ref, g)
    for a in range(3):
        halo_out[a] = sums[:, a * 128 : (a + 1) * 128]
    halo_in[1, 1] = sums[:, 128:256]

    pl.semaphore_wait(barrier, 30)

    def halo_copy(a, t):
        n = a * 3 + t
        return pltpu.make_async_remote_copy(
            src_ref=halo_out.at[a],
            dst_ref=halo_in.at[a, 2 - t],
            send_sem=hs_sem.at[n],
            recv_sem=hr_sem.at[a * 3 + 2 - t],
            device_id=(g, halo_seq[t], halo_frame[a]),
            device_id_type=pl.DeviceIdType.MESH,
        )

    halo = [(a, t) for a in range(3) for t in range(3) if (a, t) != (1, 1)]
    for a, t in halo:
        halo_copy(a, t).start()

    for c in fetch[2:]:
        c.wait()
    res[...] = jnp.zeros_like(res)
    rr[...] = jnp.zeros_like(rr)
    step = 512

    def fold(k, _):
        cols = pl.ds(pl.multiple_of(k * step, step), step)
        e = emb_ref[:, cols]
        gain = 1.0 + scale_ref[:, cols]
        eb = ebias_ref[:, cols]
        e_hi, e_lo = hi_lo(e.astype(f32) * gain)
        rest = jnp.concatenate([eb * gain, shift_ref[:, cols], jnp.zeros((6, step), f32)], axis=0)
        rest_hi, rest_lo = hi_lo(rest)
        rest2 = jnp.concatenate([rest_hi.astype(f32), rest_lo.astype(f32)], axis=0).astype(bf16)
        lhs = jnp.concatenate([e_hi, e_lo, rest2], axis=0)
        w = jnp.concatenate([w_ref[j, cols, :] for j in range(3)], axis=1)
        res[...] += jnp.dot(lhs, w, preferred_element_type=f32)
        b_hi = eb.astype(bf16).astype(f32)
        bias = jnp.concatenate([b_hi, eb - b_hi, jnp.zeros((14, step), f32)], axis=0).astype(bf16)
        both = jnp.concatenate([e, bias, jnp.zeros((48, step), bf16)], axis=0)
        rr[...] += nt_dot(both, both)
        return 0

    lax.fori_loop(0, D // step, fold, 0)

    lane = lax.broadcasted_iota(jnp.int32, (128, 128), 1)
    row = lax.broadcasted_iota(jnp.int32, (128, 128), 0)
    low = lane < 64
    for j in range(3):
        cols = slice(j * 128, (j + 1) * 128)
        top = res[0:64, cols] + res[64:128, cols]
        rest = res[128:136, cols] + res[136:144, cols]
        if j == 2:
            row8 = lax.broadcasted_iota(jnp.int32, (8, 128), 0)
            rest = jnp.where(row8 == 2, rest[0:1, :], rest)
            m = jnp.concatenate([top, rest, jnp.zeros((56, 128), f32)], axis=0)
            hi, lo = hi_lo(m)
            wv[0:128] = hi
            wv[128:256] = hi
            wv[256:384] = lo
            continue
        m = jnp.concatenate([top, rest, jnp.zeros((56, 128), f32)], axis=0)
        mt = m.T
        a_t = jnp.where(low, mt, 0.0)
        a_s = pltpu.roll(a_t, 64, 1)
        for half, v in ((0, a_t), (1, a_s)):
            hi, lo = hi_lo(v)
            n = (j * 2 + half) * 128
            wkv[n : n + 128, 0:128] = hi
            wkv[n : n + 128, 128:256] = lo
        if j == 1:
            bias_k[0] = jnp.broadcast_to(mt[:, 64:65], (128, 128))
            bias_k[1] = jnp.broadcast_to(mt[:, 65:66], (128, 128))
    gram = rr[...]
    g_t = jnp.where(low & (row < 64), gram, 0.0)
    gblock = g_t + pltpu.roll(pltpu.roll(g_t, 64, 1), 64, 0)
    hi, lo = hi_lo(gblock)
    wkv[512:640, 0:128] = hi
    wkv[512:640, 128:256] = lo
    wkv[640:768, 0:128] = jnp.where(lane == row, 1.0, 0.0).astype(bf16)
    wkv[640:768, 128:256] = jnp.zeros((128, 128), bf16)
    grow = gram[64:65, :] + gram[65:66, :]
    lane1 = lax.broadcasted_iota(jnp.int32, (1, 128), 1)
    bb = jnp.sum(jnp.where((lane1 == 64) | (lane1 == 65), grow, 0.0), axis=1, keepdims=True)
    grow64 = jnp.where(lane1 < 64, grow, 0.0)
    grow2 = 2.0 * (grow64 + pltpu.roll(grow64, 64, 1))
    gc = gram[:, 64:65] + gram[:, 65:66]
    gc2 = 2.0 * jnp.broadcast_to(jnp.concatenate([gc[0:64], gc[0:64]], axis=0), (128, 128))
    gcol[...] = gc2
    vt[64:128, :] = jnp.zeros((64, 10240), bf16)
    acc[...] = jnp.zeros_like(acc)

    for a, t in halo:
        halo_copy(a, t).wait_recv()
    lane24 = lax.broadcasted_iota(jnp.int32, (24, 128), 1)
    zero24 = jnp.zeros((24, 128), f32)
    has = (f > 0, None, f < 7)
    side = []
    for t in range(3):
        total = None
        for a in range(3):
            v = halo_in[a, t]
            if has[a] is not None:
                v = jnp.where(has[a], v, zero24)
            total = v if total is None else total + v
        side.append(total)
    from_left = jnp.where(s > 0, side[0], zero24)
    from_right = jnp.where(s < 31, side[2], zero24)
    ext = jnp.where((lane24 // 16) % 2 == 0, from_left, from_right)
    lat = side[1] + pltpu.roll(ext, 64, 1)
    cb = jnp.concatenate([cbias_ref[...]] * 8, axis=1)
    lat = (lat + cb).astype(bf16).astype(f32)
    mine = jnp.where(g == 0, lat[0:20], lat[4:24])
    first = mine[0:10]
    second = pltpu.roll(mine[10:20], 64, 1)
    packed = jnp.where(lax.broadcasted_iota(jnp.int32, (10, 128), 1) < 64, first, second)
    packed = jnp.concatenate([packed, jnp.zeros((6, 128), f32)], axis=0).astype(bf16)
    ysend[...] = packed
    ybuf[f] = packed

    def y_copy(i):
        ff = lax.rem(f + i, 8)
        return pltpu.make_async_remote_copy(
            src_ref=ysend, dst_ref=ybuf.at[f], send_sem=ys_sem.at[i], recv_sem=yr_sem.at[i],
            device_id=(g, s, ff), device_id_type=pl.DeviceIdType.MESH,
        )

    for i in range(1, 8):
        y_copy(i).start()

    def y_arrived(i):
        ff = lax.rem(f + 8 - i, 8)
        return pltpu.make_async_remote_copy(
            src_ref=ysend, dst_ref=ybuf.at[ff], send_sem=ys_sem.at[i], recv_sem=yr_sem.at[i],
            device_id=(g, s, ff), device_id_type=pl.DeviceIdType.MESH,
        )

    for i in range(1, 8):
        y_arrived(i).wait_recv()
    for n in range(8):
        dens[n * 10 : n * 10 + 10, :] = ybuf[n, 0:10, :].astype(f32)
    gat[z, x, core] = dens[...].astype(bf16)

    def at(n):
        if n == 0:
            return z
        return jnp.where(z > n - 1, n - 1, n)

    def z_copy(i, zz):
        return pltpu.make_async_remote_copy(
            src_ref=gat.at[z, x, core], dst_ref=gat.at[z, x, core], send_sem=zs_sem.at[i], recv_sem=zr_sem.at[i],
            device_id=z_dev(zz), device_id_type=pl.DeviceIdType.MESH,
        )

    def z_arrived(n):
        i = lax.rem(z + 8 - at(n), 8)
        return pltpu.make_async_remote_copy(
            src_ref=gat.at[z, x, core], dst_ref=gat.at[at(n), x, core], send_sem=zs_sem.at[i], recv_sem=zr_sem.at[i],
            device_id=z_dev(at(n)), device_id_type=pl.DeviceIdType.MESH,
        )

    def x_copy(n, d):
        piece = gat.at[at(n), x, core]
        return pltpu.make_async_remote_copy(
            src_ref=piece, dst_ref=piece, send_sem=xs_sem.at[n, d], recv_sem=xr_sem.at[at(n), d],
            device_id=x_dev(lax.rem(x + d, 4)), device_id_type=pl.DeviceIdType.MESH,
        )

    def x_arrived(n, d):
        xx = lax.rem(x + 4 - d, 4)
        piece = gat.at[at(n), xx, core]
        return pltpu.make_async_remote_copy(
            src_ref=piece, dst_ref=piece, send_sem=xs_sem.at[n, d], recv_sem=xr_sem.at[at(n), d],
            device_id=x_dev(xx), device_id_type=pl.DeviceIdType.MESH,
        )

    def c_copy(n, d, cc):
        xx = lax.rem(x + d, 4)
        piece = gat.at[at(n), xx, cc]
        return pltpu.make_async_remote_copy(
            src_ref=piece, dst_ref=piece, send_sem=cs_sem.at[n, d], recv_sem=cr_sem.at[n, d],
            device_id=partner, device_id_type=pl.DeviceIdType.MESH,
        )

    def spread(n):
        if n > 0:
            z_arrived(n).wait_recv()
        for d in (2, 1, 3):
            x_copy(n, d).start()
        c_copy(n, 0, core).start()

    def share(n):
        for d in (1, 3, 2):
            x_arrived(n, d).wait_recv()
            c_copy(n, 4 - d, core).start()

    def complete(n):
        for d in range(4):
            c_copy(n, d, 1 - core).wait_recv()

    def keys(*pieces):
        rows = jnp.concatenate([gat[at(n)].reshape(640, 128) for n in pieces], axis=0)
        size = 640 * len(pieces)
        wide = size // 128
        p2 = jnp.concatenate([rows, rows], axis=1)
        out = nt_dot(wkv[256:768, :], p2)
        pt = out[384:512]
        y = (out[256:384] + jnp.concatenate([gcol[...]] * wide, axis=1)) * pt
        row16 = lax.broadcasted_iota(jnp.int32, (16, size), 0)
        for half in range(2):
            ms = jnp.sum(y[half * 64 : half * 64 + 64], axis=0, keepdims=True) + bb
            inv = lax.rsqrt(jnp.maximum(ms, 0.0) * (1.0 / D) + EPS)
            kr = out[half * 128 : half * 128 + 128]
            kr = (kr + jnp.concatenate([bias_k[0]] * wide, axis=1)) * inv + jnp.concatenate([bias_k[1]] * wide, axis=1)
            ks = lax.rsqrt(jnp.sum(kr * kr, axis=0, keepdims=True) * (1.0 / 128) + EPS)
            first = pieces[0] * 1280 + half * size
            cols = slice(first, first + size)
            kt[:, cols] = (kr * ks).astype(bf16)
            vt[0:64, cols] = (pt[half * 64 : half * 64 + 64] * inv).astype(bf16)
            inv_hi = inv.astype(bf16).astype(f32)
            extra = jnp.where(row16 == 0, inv_hi, jnp.where(row16 == 1, 1.0, jnp.where(row16 == 2, inv - inv_hi, 0.0)))
            vt[64:80, cols] = extra.astype(bf16)

    def attend(half, *pieces):
        rows = slice(half * 160, half * 160 + 160)
        cols = slice(pieces[0] * 1280, pieces[-1] * 1280 + 1280)
        w = jnp.exp2(jnp.dot(q[rows], kt[:, cols], preferred_element_type=f32))
        acc[rows] += nt_dot(w.astype(bf16), vt[:, cols])

    for i in (1, 7, 2, 6, 3, 5, 4):
        z_copy(i, lax.rem(z + i, 8)).start()
    spread(0)
    for n in range(1, 8):
        spread(n)
    share(0)
    share(1)
    share(2)
    complete(0)
    keys(0)
    share(3)
    complete(1)
    keys(1)
    share(4)
    complete(2)
    keys(2)
    share(5)
    complete(3)
    keys(3)
    share(6)
    complete(4)
    keys(4)
    share(7)
    complete(5)
    complete(6)
    keys(5, 6)
    complete(7)
    fq, gq, hq = s // 4, z % 2, core
    pick_row = lax.broadcasted_iota(jnp.int32, (16, 80), 0)
    pick_col = lax.broadcasted_iota(jnp.int32, (16, 80), 1)
    pick = jnp.where((pick_row < 10) & (pick_col == pick_row + fq * 10), 1.0, 0.0).astype(bf16)
    for hx in range(2):
        blocks = [gat[zz, hx * 2 + gq, cc] for zz in range(8) for cc in range(2)]
        picked = jnp.dot(pick, jnp.concatenate(blocks, axis=1), preferred_element_type=f32)
        for n in range(16):
            qscr[hx * 16 + n] = picked[:, n * 128 : (n + 1) * 128]
    qall = qscr[...]
    for i in range(10):
        qrows[i * 32 : (i + 1) * 32, :] = qall[:, i, :]
    qp = qrows[...]
    qb = qp.astype(bf16)
    q2 = jnp.concatenate([qb, qb], axis=1)
    wq = jnp.where(hq == 0, wkv[0:128, :].astype(f32), wkv[128:256, :].astype(f32)).astype(bf16)
    raw = nt_dot(q2, wq)
    gp = nt_dot(q2, wkv[512:640, :])
    lane320 = lax.broadcasted_iota(jnp.int32, (320, 128), 1)
    y = jnp.where(lane320 // 64 == hq, (gp + grow2) * qp, 0.0)
    ms = jnp.sum(y, axis=1, keepdims=True) + bb
    inv = lax.rsqrt(jnp.maximum(ms, 0.0) * (1.0 / D) + EPS)
    c_q = res[128:129, 0:128] + res[136:137, 0:128]
    d_q = res[129:130, 0:128] + res[137:138, 0:128]
    qr = (raw + c_q) * inv + d_q
    qs = lax.rsqrt(jnp.sum(qr * qr, axis=1, keepdims=True) * (1.0 / 128) + EPS)
    q = (qr * qs * (qg_ref[...] * kg_ref[...] * (math.log2(math.e) / math.sqrt(128.0)))).astype(bf16)
    def a_copy(i, src, slot, j):
        return pltpu.make_async_remote_copy(
            src_ref=asend.at[src], dst_ref=arecv.at[slot], send_sem=as_sem.at[i], recv_sem=ar_sem.at[i],
            device_id=(j // 8, s, j % 8), device_id_type=pl.DeviceIdType.MESH,
        )

    pad = jnp.zeros((12, 128), f32)

    def finish(half):
        u = acc[half * 160 : half * 160 + 160]
        hi, lo = hi_lo(u)
        numer = jnp.dot(jnp.concatenate([hi, lo, hi], axis=1), wv[...], preferred_element_type=f32)
        out = numer / u[:, 65:66]
        for n in range(8):
            piece = jnp.concatenate([out[n * 20 : n * 20 + 20], pad], axis=0)
            asend[half * 8 + n] = piece.astype(bf16)

        def send_head(k, _):
            j = half * 8 + lax.rem(f + k, 8)

            @pl.when(j != head)
            def _():
                a_copy(lax.rem(j - head + 16, 16), j, head, j).start()

            return 0

        lax.fori_loop(0, 8, send_head, 0)

    attend(0, 0, 1)
    attend(0, 2, 3)
    keys(7)
    attend(0, 4, 5)
    attend(0, 6, 7)
    finish(0)
    for first in (0, 2, 4, 6):
        attend(1, first, first + 1)
    finish(1)
    arecv[head] = asend[head]

    for a, t in halo:
        halo_copy(a, t).wait_send()
    for i in range(1, 8):
        y_copy(i).wait_send()
        z_copy(i, lax.rem(z + i, 8)).wait_send()
    for n in range(8):
        for d in range(1, 4):
            x_copy(n, d).wait_send()
        for d in range(4):
            c_copy(n, d, core).wait_send()

    def head_arrived(i, _):
        j = lax.rem(head + 16 - i, 16)
        a_copy(i, j, j, j).wait_recv()
        return 0

    lax.fori_loop(1, 16, head_arrived, 0)

    def head_sent(i, _):
        j = lax.rem(head + i, 16)
        a_copy(i, j, head, j).wait_send()
        return 0

    lax.fori_loop(1, 16, head_sent, 0)


def local(
    enc_features, conv_weight, conv_bias, embed_weight, embed_bias, mod_shift, mod_scale, qkv_weight, q_gain, k_gain
):
    vmem = pl.BlockSpec(memory_space=pltpu.VMEM)
    hbm = pl.BlockSpec(memory_space=pltpu.HBM)
    dma = pltpu.SemaphoreType.DMA
    out = pl.pallas_call(
        kernel,
        out_shape=jax.ShapeDtypeStruct((16, 32, 128), bf16),
        in_specs=[hbm] * 10,
        out_specs=vmem,
        scratch_shapes=[
            pltpu.VMEM((80, 2, 512), bf16),
            pltpu.VMEM((432, 512), bf16),
            pltpu.VMEM((1, 16), f32),
            pltpu.VMEM((64, D), bf16),
            pltpu.VMEM((1, D), f32),
            pltpu.VMEM((1, D), f32),
            pltpu.VMEM((1, D), f32),
            pltpu.VMEM((3, D, 128), bf16),
            pltpu.VMEM((1, 128), f32),
            pltpu.VMEM((1, 128), f32),
            pltpu.VMEM((3, 24, 128), f32),
            pltpu.VMEM((3, 3, 24, 128), f32),
            pltpu.VMEM((8, 16, 128), bf16),
            pltpu.VMEM((16, 128), bf16),
            pltpu.VMEM((80, 128), f32),
            pltpu.VMEM((8, 4, 2, 80, 128), bf16),
            pltpu.VMEM((144, 384), f32),
            pltpu.VMEM((128, 128), f32),
            pltpu.VMEM((768, 256), bf16),
            pltpu.VMEM((384, 128), bf16),
            pltpu.VMEM((2, 128, 128), f32),
            pltpu.VMEM((128, 128), f32),
            pltpu.VMEM((128, 10240), bf16),
            pltpu.VMEM((128, 10240), bf16),
            pltpu.VMEM((32, 16, 128), f32),
            pltpu.VMEM((320, 128), f32),
            pltpu.VMEM((320, 128), f32),
            pltpu.VMEM((16, 32, 128), bf16),
            dma((10,)),
            dma((9,)),
            dma((9,)),
            dma((8,)),
            dma((8,)),
            dma((8,)),
            dma((8,)),
            dma((8, 4)),
            dma((8, 4)),
            dma((8, 4)),
            dma((8, 4)),
            dma((16,)),
            dma((16,)),
        ],
        compiler_params=pltpu.CompilerParams(
            collective_id=0, has_side_effects=True, vmem_limit_bytes=60 * 1024 * 1024
        ),
        cost_estimate=pl.CostEstimate(flops=5_000_000_000, bytes_accessed=6_000_000, transcendentals=3_300_000),
    )(
        enc_features.reshape(80, 2, 512),
        conv_weight.transpose(0, 1, 2, 4, 3).reshape(432, 512),
        conv_bias.reshape(1, 16),
        embed_weight,
        embed_bias.reshape(1, D),
        mod_shift.reshape(1, D),
        mod_scale.reshape(1, D),
        qkv_weight.transpose(1, 2, 0, 3).reshape(3, D, 128),
        q_gain.reshape(1, 128),
        k_gain.reshape(1, 128),
    )
    return out[:, :20, :].transpose(1, 0, 2).reshape(1, 1, 20, 2048)


def solution(mesh):
    in_specs = (
        P("tile", None, "seq", None), P(), P(), P(), P(), P(), P(), P(None, None, ("grp", "tile"), None), P(), P(),
    )
    out_specs = P("seq", ("grp", "tile"), None, None)
    return jax.shard_map(local, mesh=mesh, in_specs=in_specs, out_specs=out_specs, check_vma=False)
```

```python
import math

import jax
import jax.numpy as jnp
from jax import lax
from jax.experimental import pallas as pl
from jax.experimental.pallas import tpu as pltpu
from jax.sharding import PartitionSpec as P

bf16 = jnp.bfloat16
f32 = jnp.float32

D = 4096
NT = (((1,), (1,)), ((), ()))
EPS = 1e-6


def nt_dot(a, b):
    return lax.dot_general(a, b, NT, preferred_element_type=f32)


def hi_lo(v):
    hi = v.astype(bf16)
    return hi, (v - hi.astype(f32)).astype(bf16)


def conv_block(cw_ref, rho, col):
    zero = jnp.zeros((16, 512), bf16)
    pieces = []
    for a in range(3):
        for ext in range(2):
            for p in range(2):
                for q in range(2):
                    b = rho - p
                    rel = q if ext == 0 else (2 if q == 0 else -1)
                    e = col - rel + 1
                    if 0 <= b <= 2 and 0 <= e <= 2:
                        r = ((a * 3 + b) * 3 + e) * 16
                        pieces.append(cw_ref[r : r + 16, :])
                    else:
                        pieces.append(zero)
    return jnp.concatenate(pieces, axis=0)


def conv_partials(x_ref, cw_ref, g):
    v = x_ref[...].astype(f32).reshape(40, 4, 512)
    part = [v[:, j, :] for j in range(4)]
    edge = jnp.zeros((1, 512), f32)
    acc = None
    for rho in range(4):
        for col in range(2):
            if rho == 0:
                rows = jnp.concatenate([edge, part[2 + col][:39]], axis=0)
            elif rho == 3:
                rows = jnp.concatenate([part[col][1:], edge], axis=0)
            else:
                rows = part[(rho - 1) * 2 + col]
            rows = jnp.where(g == 0, rows[0:24], rows[16:40]).astype(bf16)
            term = nt_dot(rows, conv_block(cw_ref, rho, col))
            acc = term if acc is None else acc + term
    return acc


def kernel(
    x_hbm, cw_hbm, cbias_hbm, emb_hbm, ebias_hbm, shift_hbm, scale_hbm, w_hbm, qg_hbm, kg_hbm,
    arecv,
    x_ref, cw_ref, cbias_ref, emb_ref, ebias_ref, shift_ref, scale_ref, w_ref, qg_ref, kg_ref, halo_out, halo_in, ybuf, ysend, dens, gat, res, rr, wkv, wv, bias_k, gcol,
    kt, vt, qscr, qrows, acc, asend,
    local_sem, hs_sem, hr_sem, ys_sem, yr_sem, zs_sem, zr_sem, xs_sem, xr_sem, cs_sem, cr_sem,
    as_sem, ar_sem,
):
    g = lax.axis_index("grp")
    s = lax.axis_index("seq")
    f = lax.axis_index("tile")
    xh, z, core = s // 16, (s // 2) % 8, s % 2
    x = xh * 2 + g
    head = g * 8 + f

    def dev(gg, ss, ff):
        return (gg, ss, ff)

    def x_dev(xx):
        return (xx % 2, (xx // 2) * 16 + z * 2 + core, f)

    def z_dev(zz):
        return (g, xh * 16 + zz * 2 + core, f)

    left, right = lax.rem(s + 31, 32), lax.rem(s + 1, 32)
    before, after = lax.rem(f + 7, 8), lax.rem(f + 1, 8)
    xm, xp, xo = lax.rem(x + 3, 4), lax.rem(x + 1, 4), lax.rem(x + 2, 4)
    partner = (g, s + 1 - 2 * core, f)
    halo_seq = (left, s, right)
    halo_frame = (after, f, before)

    pairs = (
        (x_hbm, x_ref), (cw_hbm, cw_ref), (cbias_hbm, cbias_ref), (emb_hbm, emb_ref), (ebias_hbm, ebias_ref),
        (shift_hbm, shift_ref), (scale_hbm, scale_ref), (w_hbm, w_ref), (qg_hbm, qg_ref), (kg_hbm, kg_ref),
    )
    fetch = [pltpu.make_async_copy(src, dst, local_sem.at[n]) for n, (src, dst) in enumerate(pairs)]
    fetch[0].start()
    fetch[1].start()

    barrier = pltpu.get_barrier_semaphore()

    def greet(device):
        pl.semaphore_signal(barrier, inc=1, device_id=device, device_id_type=pl.DeviceIdType.MESH)

    for ss in (left, right):
        for ff in halo_frame:
            greet((g, ss, ff))

    def greet_z(i, _):
        greet(z_dev(lax.rem(z + i, 8)))
        return 0

    lax.fori_loop(1, 8, greet_z, 0)

    def greet_head(i, _):
        j = lax.rem(head + i, 16)
        greet((j // 8, s, j % 8))
        return 0

    lax.fori_loop(1, 16, greet_head, 0)
    greet(x_dev(xo))
    greet(x_dev(jnp.where(g == 0, xm, xp)))

    for c in fetch[2:]:
        c.start()
    fetch[0].wait()
    fetch[1].wait()
    sums = conv_partials(x_ref, cw_ref, g)
    for a in range(3):
        halo_out[a] = sums[:, a * 128 : (a + 1) * 128]
    halo_in[1, 1] = sums[:, 128:256]

    pl.semaphore_wait(barrier, 30)

    def halo_copy(a, t):
        n = a * 3 + t
        return pltpu.make_async_remote_copy(
            src_ref=halo_out.at[a],
            dst_ref=halo_in.at[a, 2 - t],
            send_sem=hs_sem.at[n],
            recv_sem=hr_sem.at[a * 3 + 2 - t],
            device_id=(g, halo_seq[t], halo_frame[a]),
            device_id_type=pl.DeviceIdType.MESH,
        )

    halo = [(a, t) for a in range(3) for t in range(3) if (a, t) != (1, 1)]
    for a, t in halo:
        halo_copy(a, t).start()

    for c in fetch[2:]:
        c.wait()
    res[...] = jnp.zeros_like(res)
    rr[...] = jnp.zeros_like(rr)
    step = 512

    def fold(k, _):
        cols = pl.ds(pl.multiple_of(k * step, step), step)
        e = emb_ref[:, cols]
        gain = 1.0 + scale_ref[:, cols]
        eb = ebias_ref[:, cols]
        e_hi, e_lo = hi_lo(e.astype(f32) * gain)
        rest = jnp.concatenate([eb * gain, shift_ref[:, cols], jnp.zeros((6, step), f32)], axis=0)
        rest_hi, rest_lo = hi_lo(rest)
        rest2 = jnp.concatenate([rest_hi.astype(f32), rest_lo.astype(f32)], axis=0).astype(bf16)
        lhs = jnp.concatenate([e_hi, e_lo, rest2], axis=0)
        w = jnp.concatenate([w_ref[j, cols, :] for j in range(3)], axis=1)
        res[...] += jnp.dot(lhs, w, preferred_element_type=f32)
        b_hi = eb.astype(bf16).astype(f32)
        bias = jnp.concatenate([b_hi, eb - b_hi, jnp.zeros((14, step), f32)], axis=0).astype(bf16)
        both = jnp.concatenate([e, bias, jnp.zeros((48, step), bf16)], axis=0)
        rr[...] += nt_dot(both, both)
        return 0

    lax.fori_loop(0, D // step, fold, 0)

    lane = lax.broadcasted_iota(jnp.int32, (128, 128), 1)
    row = lax.broadcasted_iota(jnp.int32, (128, 128), 0)
    low = lane < 64
    for j in range(3):
        cols = slice(j * 128, (j + 1) * 128)
        top = res[0:64, cols] + res[64:128, cols]
        rest = res[128:136, cols] + res[136:144, cols]
        if j == 2:
            row8 = lax.broadcasted_iota(jnp.int32, (8, 128), 0)
            rest = jnp.where(row8 == 2, rest[0:1, :], rest)
            m = jnp.concatenate([top, rest, jnp.zeros((56, 128), f32)], axis=0)
            hi, lo = hi_lo(m)
            wv[0:128] = hi
            wv[128:256] = hi
            wv[256:384] = lo
            continue
        m = jnp.concatenate([top, rest, jnp.zeros((56, 128), f32)], axis=0)
        mt = m.T
        a_t = jnp.where(low, mt, 0.0)
        a_s = pltpu.roll(a_t, 64, 1)
        for half, v in ((0, a_t), (1, a_s)):
            hi, lo = hi_lo(v)
            n = (j * 2 + half) * 128
            wkv[n : n + 128, 0:128] = hi
            wkv[n : n + 128, 128:256] = lo
        if j == 1:
            bias_k[0] = jnp.broadcast_to(mt[:, 64:65], (128, 128))
            bias_k[1] = jnp.broadcast_to(mt[:, 65:66], (128, 128))
    gram = rr[...]
    g_t = jnp.where(low & (row < 64), gram, 0.0)
    gblock = g_t + pltpu.roll(pltpu.roll(g_t, 64, 1), 64, 0)
    hi, lo = hi_lo(gblock)
    wkv[512:640, 0:128] = hi
    wkv[512:640, 128:256] = lo
    wkv[640:768, 0:128] = jnp.where(lane == row, 1.0, 0.0).astype(bf16)
    wkv[640:768, 128:256] = jnp.zeros((128, 128), bf16)
    grow = gram[64:65, :] + gram[65:66, :]
    lane1 = lax.broadcasted_iota(jnp.int32, (1, 128), 1)
    bb = jnp.sum(jnp.where((lane1 == 64) | (lane1 == 65), grow, 0.0), axis=1, keepdims=True)
    grow64 = jnp.where(lane1 < 64, grow, 0.0)
    grow2 = 2.0 * (grow64 + pltpu.roll(grow64, 64, 1))
    gc = gram[:, 64:65] + gram[:, 65:66]
    gc2 = 2.0 * jnp.broadcast_to(jnp.concatenate([gc[0:64], gc[0:64]], axis=0), (128, 128))
    gcol[...] = gc2
    vt[64:128, :] = jnp.zeros((64, 10240), bf16)
    acc[...] = jnp.zeros_like(acc)

    for a, t in halo:
        halo_copy(a, t).wait_recv()
    lane24 = lax.broadcasted_iota(jnp.int32, (24, 128), 1)
    zero24 = jnp.zeros((24, 128), f32)
    has = (f > 0, None, f < 7)
    side = []
    for t in range(3):
        total = None
        for a in range(3):
            v = halo_in[a, t]
            if has[a] is not None:
                v = jnp.where(has[a], v, zero24)
            total = v if total is None else total + v
        side.append(total)
    from_left = jnp.where(s > 0, side[0], zero24)
    from_right = jnp.where(s < 31, side[2], zero24)
    ext = jnp.where((lane24 // 16) % 2 == 0, from_left, from_right)
    lat = side[1] + pltpu.roll(ext, 64, 1)
    cb = jnp.concatenate([cbias_ref[...]] * 8, axis=1)
    lat = (lat + cb).astype(bf16).astype(f32)
    mine = jnp.where(g == 0, lat[0:20], lat[4:24])
    first = mine[0:10]
    second = pltpu.roll(mine[10:20], 64, 1)
    packed = jnp.where(lax.broadcasted_iota(jnp.int32, (10, 128), 1) < 64, first, second)
    packed = jnp.concatenate([packed, jnp.zeros((6, 128), f32)], axis=0).astype(bf16)
    ysend[...] = packed
    ybuf[f] = packed

    def y_copy(i):
        ff = lax.rem(f + i, 8)
        return pltpu.make_async_remote_copy(
            src_ref=ysend, dst_ref=ybuf.at[f], send_sem=ys_sem.at[i], recv_sem=yr_sem.at[i],
            device_id=(g, s, ff), device_id_type=pl.DeviceIdType.MESH,
        )

    for i in range(1, 8):
        y_copy(i).start()

    def y_arrived(i):
        ff = lax.rem(f + 8 - i, 8)
        return pltpu.make_async_remote_copy(
            src_ref=ysend, dst_ref=ybuf.at[ff], send_sem=ys_sem.at[i], recv_sem=yr_sem.at[i],
            device_id=(g, s, ff), device_id_type=pl.DeviceIdType.MESH,
        )

    for i in range(1, 8):
        y_arrived(i).wait_recv()
    for n in range(8):
        dens[n * 10 : n * 10 + 10, :] = ybuf[n, 0:10, :].astype(f32)
    gat[z, x, core] = dens[...].astype(bf16)

    def at(n):
        if n == 0:
            return z
        return jnp.where(z > n - 1, n - 1, n)

    def z_copy(i, zz):
        return pltpu.make_async_remote_copy(
            src_ref=gat.at[z, x, core], dst_ref=gat.at[z, x, core], send_sem=zs_sem.at[i], recv_sem=zr_sem.at[i],
            device_id=z_dev(zz), device_id_type=pl.DeviceIdType.MESH,
        )

    def z_arrived(n):
        i = lax.rem(z + 8 - at(n), 8)
        return pltpu.make_async_remote_copy(
            src_ref=gat.at[z, x, core], dst_ref=gat.at[at(n), x, core], send_sem=zs_sem.at[i], recv_sem=zr_sem.at[i],
            device_id=z_dev(at(n)), device_id_type=pl.DeviceIdType.MESH,
        )

    def x_copy(n, d):
        piece = gat.at[at(n), x, core]
        return pltpu.make_async_remote_copy(
            src_ref=piece, dst_ref=piece, send_sem=xs_sem.at[n, d], recv_sem=xr_sem.at[at(n), d],
            device_id=x_dev(lax.rem(x + d, 4)), device_id_type=pl.DeviceIdType.MESH,
        )

    def x_arrived(n, d):
        xx = lax.rem(x + 4 - d, 4)
        piece = gat.at[at(n), xx, core]
        return pltpu.make_async_remote_copy(
            src_ref=piece, dst_ref=piece, send_sem=xs_sem.at[n, d], recv_sem=xr_sem.at[at(n), d],
            device_id=x_dev(xx), device_id_type=pl.DeviceIdType.MESH,
        )

    def c_copy(n, d, cc):
        xx = lax.rem(x + d, 4)
        piece = gat.at[at(n), xx, cc]
        return pltpu.make_async_remote_copy(
            src_ref=piece, dst_ref=piece, send_sem=cs_sem.at[n, d], recv_sem=cr_sem.at[n, d],
            device_id=partner, device_id_type=pl.DeviceIdType.MESH,
        )

    def spread(n):
        if n > 0:
            z_arrived(n).wait_recv()
        for d in (2, 1, 3):
            x_copy(n, d).start()
        c_copy(n, 0, core).start()

    def share(n):
        for d in (1, 3, 2):
            x_arrived(n, d).wait_recv()
            c_copy(n, 4 - d, core).start()

    def complete(n):
        for d in range(4):
            c_copy(n, d, 1 - core).wait_recv()

    def keys(*pieces):
        rows = jnp.concatenate([gat[at(n)].reshape(640, 128) for n in pieces], axis=0)
        size = 640 * len(pieces)
        wide = size // 128
        p2 = jnp.concatenate([rows, rows], axis=1)
        out = nt_dot(wkv[256:768, :], p2)
        pt = out[384:512]
        y = (out[256:384] + jnp.concatenate([gcol[...]] * wide, axis=1)) * pt
        row16 = lax.broadcasted_iota(jnp.int32, (16, size), 0)
        for half in range(2):
            ms = jnp.sum(y[half * 64 : half * 64 + 64], axis=0, keepdims=True) + bb
            inv = lax.rsqrt(jnp.maximum(ms, 0.0) * (1.0 / D) + EPS)
            kr = out[half * 128 : half * 128 + 128]
            kr = (kr + jnp.concatenate([bias_k[0]] * wide, axis=1)) * inv + jnp.concatenate([bias_k[1]] * wide, axis=1)
            ks = lax.rsqrt(jnp.sum(kr * kr, axis=0, keepdims=True) * (1.0 / 128) + EPS)
            first = pieces[0] * 1280 + half * size
            cols = slice(first, first + size)
            kt[:, cols] = (kr * ks).astype(bf16)
            vt[0:64, cols] = (pt[half * 64 : half * 64 + 64] * inv).astype(bf16)
            inv_hi = inv.astype(bf16).astype(f32)
            extra = jnp.where(row16 == 0, inv_hi, jnp.where(row16 == 1, 1.0, jnp.where(row16 == 2, inv - inv_hi, 0.0)))
            vt[64:80, cols] = extra.astype(bf16)

    def attend(half, *pieces):
        rows = slice(half * 160, half * 160 + 160)
        cols = slice(pieces[0] * 1280, pieces[-1] * 1280 + 1280)
        w = jnp.exp2(jnp.dot(q[rows], kt[:, cols], preferred_element_type=f32))
        acc[rows] += nt_dot(w.astype(bf16), vt[:, cols])

    for i in (1, 7, 2, 6, 3, 5, 4):
        z_copy(i, lax.rem(z + i, 8)).start()
    spread(0)
    for n in range(1, 8):
        spread(n)
    share(0)
    share(1)
    share(2)
    complete(0)
    keys(0)
    share(3)
    complete(1)
    keys(1)
    share(4)
    complete(2)
    keys(2)
    share(5)
    complete(3)
    keys(3)
    share(6)
    complete(4)
    keys(4)
    share(7)
    complete(5)
    complete(6)
    keys(5, 6)
    complete(7)
    fq, gq, hq = s // 4, z % 2, core
    pick_row = lax.broadcasted_iota(jnp.int32, (16, 80), 0)
    pick_col = lax.broadcasted_iota(jnp.int32, (16, 80), 1)
    pick = jnp.where((pick_row < 10) & (pick_col == pick_row + fq * 10), 1.0, 0.0).astype(bf16)
    for hx in range(2):
        blocks = [gat[zz, hx * 2 + gq, cc] for zz in range(8) for cc in range(2)]
        picked = jnp.dot(pick, jnp.concatenate(blocks, axis=1), preferred_element_type=f32)
        for n in range(16):
            qscr[hx * 16 + n] = picked[:, n * 128 : (n + 1) * 128]
    qall = qscr[...]
    for i in range(10):
        qrows[i * 32 : (i + 1) * 32, :] = qall[:, i, :]
    qp = qrows[...]
    qb = qp.astype(bf16)
    q2 = jnp.concatenate([qb, qb], axis=1)
    wq = jnp.where(hq == 0, wkv[0:128, :].astype(f32), wkv[128:256, :].astype(f32)).astype(bf16)
    raw = nt_dot(q2, wq)
    gp = nt_dot(q2, wkv[512:640, :])
    lane320 = lax.broadcasted_iota(jnp.int32, (320, 128), 1)
    y = jnp.where(lane320 // 64 == hq, (gp + grow2) * qp, 0.0)
    ms = jnp.sum(y, axis=1, keepdims=True) + bb
    inv = lax.rsqrt(jnp.maximum(ms, 0.0) * (1.0 / D) + EPS)
    c_q = res[128:129, 0:128] + res[136:137, 0:128]
    d_q = res[129:130, 0:128] + res[137:138, 0:128]
    qr = (raw + c_q) * inv + d_q
    qs = lax.rsqrt(jnp.sum(qr * qr, axis=1, keepdims=True) * (1.0 / 128) + EPS)
    q = (qr * qs * (qg_ref[...] * kg_ref[...] * (math.log2(math.e) / math.sqrt(128.0)))).astype(bf16)
    def a_copy(i, src, slot, j):
        return pltpu.make_async_remote_copy(
            src_ref=asend.at[src], dst_ref=arecv.at[slot], send_sem=as_sem.at[i], recv_sem=ar_sem.at[i],
            device_id=(j // 8, s, j % 8), device_id_type=pl.DeviceIdType.MESH,
        )

    pad = jnp.zeros((12, 128), f32)

    def finish(half):
        u = acc[half * 160 : half * 160 + 160]
        hi, lo = hi_lo(u)
        numer = jnp.dot(jnp.concatenate([hi, lo, hi], axis=1), wv[...], preferred_element_type=f32)
        out = numer / u[:, 65:66]
        for n in range(8):
            piece = jnp.concatenate([out[n * 20 : n * 20 + 20], pad], axis=0)
            asend[half * 8 + n] = piece.astype(bf16)

        for k in (4, 3, 5, 2, 6, 1, 7, 0):
            j = half * 8 + lax.rem(f + k, 8)

            @pl.when(j != head)
            def _():
                a_copy(lax.rem(j - head + 16, 16), j, head, j).start()

    attend(0, 0, 1)
    attend(0, 2, 3)
    keys(7)
    attend(0, 4, 5)
    attend(0, 6, 7)
    finish(0)
    for first in (0, 2, 4, 6):
        attend(1, first, first + 1)
    finish(1)
    arecv[head] = asend[head]

    for a, t in halo:
        halo_copy(a, t).wait_send()
    for i in range(1, 8):
        y_copy(i).wait_send()
        z_copy(i, lax.rem(z + i, 8)).wait_send()
    for n in range(8):
        for d in range(1, 4):
            x_copy(n, d).wait_send()
        for d in range(4):
            c_copy(n, d, core).wait_send()

    def head_arrived(i, _):
        j = lax.rem(head + 16 - i, 16)
        a_copy(i, j, j, j).wait_recv()
        return 0

    lax.fori_loop(1, 16, head_arrived, 0)

    def head_sent(i, _):
        j = lax.rem(head + i, 16)
        a_copy(i, j, head, j).wait_send()
        return 0

    lax.fori_loop(1, 16, head_sent, 0)


def local(
    enc_features, conv_weight, conv_bias, embed_weight, embed_bias, mod_shift, mod_scale, qkv_weight, q_gain, k_gain
):
    vmem = pl.BlockSpec(memory_space=pltpu.VMEM)
    hbm = pl.BlockSpec(memory_space=pltpu.HBM)
    dma = pltpu.SemaphoreType.DMA
    out = pl.pallas_call(
        kernel,
        out_shape=jax.ShapeDtypeStruct((16, 32, 128), bf16),
        in_specs=[hbm] * 10,
        out_specs=vmem,
        scratch_shapes=[
            pltpu.VMEM((80, 2, 512), bf16),
            pltpu.VMEM((432, 512), bf16),
            pltpu.VMEM((1, 16), f32),
            pltpu.VMEM((64, D), bf16),
            pltpu.VMEM((1, D), f32),
            pltpu.VMEM((1, D), f32),
            pltpu.VMEM((1, D), f32),
            pltpu.VMEM((3, D, 128), bf16),
            pltpu.VMEM((1, 128), f32),
            pltpu.VMEM((1, 128), f32),
            pltpu.VMEM((3, 24, 128), f32),
            pltpu.VMEM((3, 3, 24, 128), f32),
            pltpu.VMEM((8, 16, 128), bf16),
            pltpu.VMEM((16, 128), bf16),
            pltpu.VMEM((80, 128), f32),
            pltpu.VMEM((8, 4, 2, 80, 128), bf16),
            pltpu.VMEM((144, 384), f32),
            pltpu.VMEM((128, 128), f32),
            pltpu.VMEM((768, 256), bf16),
            pltpu.VMEM((384, 128), bf16),
            pltpu.VMEM((2, 128, 128), f32),
            pltpu.VMEM((128, 128), f32),
            pltpu.VMEM((128, 10240), bf16),
            pltpu.VMEM((128, 10240), bf16),
            pltpu.VMEM((32, 16, 128), f32),
            pltpu.VMEM((320, 128), f32),
            pltpu.VMEM((320, 128), f32),
            pltpu.VMEM((16, 32, 128), bf16),
            dma((10,)),
            dma((9,)),
            dma((9,)),
            dma((8,)),
            dma((8,)),
            dma((8,)),
            dma((8,)),
            dma((8, 4)),
            dma((8, 4)),
            dma((8, 4)),
            dma((8, 4)),
            dma((16,)),
            dma((16,)),
        ],
        compiler_params=pltpu.CompilerParams(
            collective_id=0, has_side_effects=True, vmem_limit_bytes=60 * 1024 * 1024
        ),
        cost_estimate=pl.CostEstimate(flops=5_000_000_000, bytes_accessed=6_000_000, transcendentals=3_300_000),
    )(
        enc_features.reshape(80, 2, 512),
        conv_weight.transpose(0, 1, 2, 4, 3).reshape(432, 512),
        conv_bias.reshape(1, 16),
        embed_weight,
        embed_bias.reshape(1, D),
        mod_shift.reshape(1, D),
        mod_scale.reshape(1, D),
        qkv_weight.transpose(1, 2, 0, 3).reshape(3, D, 128),
        q_gain.reshape(1, 128),
        k_gain.reshape(1, 128),
    )
    return out[:, :20, :].transpose(1, 0, 2).reshape(1, 1, 20, 2048)


def solution(mesh):
    in_specs = (
        P("tile", None, "seq", None), P(), P(), P(), P(), P(), P(), P(None, None, ("grp", "tile"), None), P(), P(),
    )
    out_specs = P("seq", ("grp", "tile"), None, None)
    return jax.shard_map(local, mesh=mesh, in_specs=in_specs, out_specs=out_specs, check_vma=False)
```

```python
import math

import jax
import jax.numpy as jnp
from jax import lax
from jax.experimental import pallas as pl
from jax.experimental.pallas import tpu as pltpu
from jax.sharding import PartitionSpec as P

bf16 = jnp.bfloat16
f32 = jnp.float32

D = 4096
NT = (((1,), (1,)), ((), ()))
EPS = 1e-6


def nt_dot(a, b):
    return lax.dot_general(a, b, NT, preferred_element_type=f32)


def hi_lo(v):
    hi = v.astype(bf16)
    return hi, (v - hi.astype(f32)).astype(bf16)


def conv_block(cw_ref, rho, col):
    zero = jnp.zeros((16, 512), bf16)
    pieces = []
    for a in range(3):
        for ext in range(2):
            for p in range(2):
                for q in range(2):
                    b = rho - p
                    rel = q if ext == 0 else (2 if q == 0 else -1)
                    e = col - rel + 1
                    if 0 <= b <= 2 and 0 <= e <= 2:
                        r = ((a * 3 + b) * 3 + e) * 16
                        pieces.append(cw_ref[r : r + 16, :])
                    else:
                        pieces.append(zero)
    return jnp.concatenate(pieces, axis=0)


def conv_partials(x_ref, cw_ref, g):
    v = x_ref[...].astype(f32).reshape(40, 4, 512)
    part = [v[:, j, :] for j in range(4)]
    edge = jnp.zeros((1, 512), f32)
    acc = None
    for rho in range(4):
        for col in range(2):
            if rho == 0:
                rows = jnp.concatenate([edge, part[2 + col][:39]], axis=0)
            elif rho == 3:
                rows = jnp.concatenate([part[col][1:], edge], axis=0)
            else:
                rows = part[(rho - 1) * 2 + col]
            rows = jnp.where(g == 0, rows[0:24], rows[16:40]).astype(bf16)
            term = nt_dot(rows, conv_block(cw_ref, rho, col))
            acc = term if acc is None else acc + term
    return acc


def kernel(
    x_hbm, cw_hbm, cbias_hbm, emb_hbm, ebias_hbm, shift_hbm, scale_hbm, w_hbm, qg_hbm, kg_hbm,
    arecv,
    x_ref, cw_ref, cbias_ref, emb_ref, ebias_ref, shift_ref, scale_ref, w_ref, qg_ref, kg_ref, halo_out, halo_in, ybuf, ysend, dens, gat, res, rr, wkv, wv, bias_k, gcol,
    kt, vt, qscr, qrows, acc, asend,
    local_sem, hs_sem, hr_sem, ys_sem, yr_sem, zs_sem, zr_sem, xs_sem, xr_sem, cs_sem, cr_sem,
    as_sem, ar_sem,
):
    g = lax.axis_index("grp")
    s = lax.axis_index("seq")
    f = lax.axis_index("tile")
    xh, z, core = s // 16, (s // 2) % 8, s % 2
    x = xh * 2 + g
    head = g * 8 + f

    def dev(gg, ss, ff):
        return (gg, ss, ff)

    def x_dev(xx):
        return (xx % 2, (xx // 2) * 16 + z * 2 + core, f)

    def z_dev(zz):
        return (g, xh * 16 + zz * 2 + core, f)

    left, right = lax.rem(s + 31, 32), lax.rem(s + 1, 32)
    before, after = lax.rem(f + 7, 8), lax.rem(f + 1, 8)
    xm, xp, xo = lax.rem(x + 3, 4), lax.rem(x + 1, 4), lax.rem(x + 2, 4)
    partner = (g, s + 1 - 2 * core, f)
    halo_seq = (left, s, right)
    halo_frame = (after, f, before)

    pairs = (
        (x_hbm, x_ref), (cw_hbm, cw_ref), (cbias_hbm, cbias_ref), (emb_hbm, emb_ref), (ebias_hbm, ebias_ref),
        (shift_hbm, shift_ref), (scale_hbm, scale_ref), (w_hbm, w_ref), (qg_hbm, qg_ref), (kg_hbm, kg_ref),
    )
    fetch = [pltpu.make_async_copy(src, dst, local_sem.at[n]) for n, (src, dst) in enumerate(pairs)]
    fetch[0].start()
    fetch[1].start()

    barrier = pltpu.get_barrier_semaphore()

    def greet(device):
        pl.semaphore_signal(barrier, inc=1, device_id=device, device_id_type=pl.DeviceIdType.MESH)

    for ss in (left, right):
        for ff in halo_frame:
            greet((g, ss, ff))

    def greet_z(i, _):
        greet(z_dev(lax.rem(z + i, 8)))
        return 0

    lax.fori_loop(1, 8, greet_z, 0)

    def greet_head(i, _):
        j = lax.rem(head + i, 16)
        greet((j // 8, s, j % 8))
        return 0

    lax.fori_loop(1, 16, greet_head, 0)
    greet(x_dev(xo))
    greet(x_dev(jnp.where(g == 0, xm, xp)))

    for c in fetch[2:]:
        c.start()
    fetch[0].wait()
    fetch[1].wait()
    sums = conv_partials(x_ref, cw_ref, g)
    for a in range(3):
        halo_out[a] = sums[:, a * 128 : (a + 1) * 128]
    halo_in[1, 1] = sums[:, 128:256]

    pl.semaphore_wait(barrier, 30)

    def halo_copy(a, t):
        n = a * 3 + t
        return pltpu.make_async_remote_copy(
            src_ref=halo_out.at[a],
            dst_ref=halo_in.at[a, 2 - t],
            send_sem=hs_sem.at[n],
            recv_sem=hr_sem.at[a * 3 + 2 - t],
            device_id=(g, halo_seq[t], halo_frame[a]),
            device_id_type=pl.DeviceIdType.MESH,
        )

    halo = [(a, t) for a in range(3) for t in range(3) if (a, t) != (1, 1)]
    for a, t in halo:
        halo_copy(a, t).start()

    for c in fetch[2:]:
        c.wait()
    res[...] = jnp.zeros_like(res)
    rr[...] = jnp.zeros_like(rr)
    step = 512

    def fold(k, _):
        cols = pl.ds(pl.multiple_of(k * step, step), step)
        e = emb_ref[:, cols]
        gain = 1.0 + scale_ref[:, cols]
        eb = ebias_ref[:, cols]
        e_hi, e_lo = hi_lo(e.astype(f32) * gain)
        rest = jnp.concatenate([eb * gain, shift_ref[:, cols], jnp.zeros((6, step), f32)], axis=0)
        rest_hi, rest_lo = hi_lo(rest)
        rest2 = jnp.concatenate([rest_hi.astype(f32), rest_lo.astype(f32)], axis=0).astype(bf16)
        lhs = jnp.concatenate([e_hi, e_lo, rest2], axis=0)
        w = jnp.concatenate([w_ref[j, cols, :] for j in range(3)], axis=1)
        res[...] += jnp.dot(lhs, w, preferred_element_type=f32)
        b_hi = eb.astype(bf16).astype(f32)
        bias = jnp.concatenate([b_hi, eb - b_hi, jnp.zeros((14, step), f32)], axis=0).astype(bf16)
        both = jnp.concatenate([e, bias, jnp.zeros((48, step), bf16)], axis=0)
        rr[...] += nt_dot(both, both)
        return 0

    lax.fori_loop(0, D // step, fold, 0)

    lane = lax.broadcasted_iota(jnp.int32, (128, 128), 1)
    row = lax.broadcasted_iota(jnp.int32, (128, 128), 0)
    low = lane < 64
    for j in range(3):
        cols = slice(j * 128, (j + 1) * 128)
        top = res[0:64, cols] + res[64:128, cols]
        rest = res[128:136, cols] + res[136:144, cols]
        if j == 2:
            row8 = lax.broadcasted_iota(jnp.int32, (8, 128), 0)
            rest = jnp.where(row8 == 2, rest[0:1, :], rest)
            m = jnp.concatenate([top, rest, jnp.zeros((56, 128), f32)], axis=0)
            hi, lo = hi_lo(m)
            wv[0:128] = hi
            wv[128:256] = hi
            wv[256:384] = lo
            continue
        m = jnp.concatenate([top, rest, jnp.zeros((56, 128), f32)], axis=0)
        mt = m.T
        a_t = jnp.where(low, mt, 0.0)
        a_s = pltpu.roll(a_t, 64, 1)
        for half, v in ((0, a_t), (1, a_s)):
            hi, lo = hi_lo(v)
            n = (j * 2 + half) * 128
            wkv[n : n + 128, 0:128] = hi
            wkv[n : n + 128, 128:256] = lo
        if j == 1:
            bias_k[0] = jnp.broadcast_to(mt[:, 64:65], (128, 128))
            bias_k[1] = jnp.broadcast_to(mt[:, 65:66], (128, 128))
    gram = rr[...]
    g_t = jnp.where(low & (row < 64), gram, 0.0)
    gblock = g_t + pltpu.roll(pltpu.roll(g_t, 64, 1), 64, 0)
    hi, lo = hi_lo(gblock)
    wkv[512:640, 0:128] = hi
    wkv[512:640, 128:256] = lo
    wkv[640:768, 0:128] = jnp.where(lane == row, 1.0, 0.0).astype(bf16)
    wkv[640:768, 128:256] = jnp.zeros((128, 128), bf16)
    grow = gram[64:65, :] + gram[65:66, :]
    lane1 = lax.broadcasted_iota(jnp.int32, (1, 128), 1)
    bb = jnp.sum(jnp.where((lane1 == 64) | (lane1 == 65), grow, 0.0), axis=1, keepdims=True)
    grow64 = jnp.where(lane1 < 64, grow, 0.0)
    grow2 = 2.0 * (grow64 + pltpu.roll(grow64, 64, 1))
    gc = gram[:, 64:65] + gram[:, 65:66]
    gc2 = 2.0 * jnp.broadcast_to(jnp.concatenate([gc[0:64], gc[0:64]], axis=0), (128, 128))
    gcol[...] = gc2
    vt[64:128, :] = jnp.zeros((64, 10240), bf16)
    acc[...] = jnp.zeros_like(acc)

    for a, t in halo:
        halo_copy(a, t).wait_recv()
    lane24 = lax.broadcasted_iota(jnp.int32, (24, 128), 1)
    zero24 = jnp.zeros((24, 128), f32)
    has = (f > 0, None, f < 7)
    side = []
    for t in range(3):
        total = None
        for a in range(3):
            v = halo_in[a, t]
            if has[a] is not None:
                v = jnp.where(has[a], v, zero24)
            total = v if total is None else total + v
        side.append(total)
    from_left = jnp.where(s > 0, side[0], zero24)
    from_right = jnp.where(s < 31, side[2], zero24)
    ext = jnp.where((lane24 // 16) % 2 == 0, from_left, from_right)
    lat = side[1] + pltpu.roll(ext, 64, 1)
    cb = jnp.concatenate([cbias_ref[...]] * 8, axis=1)
    lat = (lat + cb).astype(bf16).astype(f32)
    mine = jnp.where(g == 0, lat[0:20], lat[4:24])
    first = mine[0:10]
    second = pltpu.roll(mine[10:20], 64, 1)
    packed = jnp.where(lax.broadcasted_iota(jnp.int32, (10, 128), 1) < 64, first, second)
    packed = jnp.concatenate([packed, jnp.zeros((6, 128), f32)], axis=0).astype(bf16)
    ysend[...] = packed
    ybuf[f] = packed

    def y_copy(i):
        ff = lax.rem(f + i, 8)
        return pltpu.make_async_remote_copy(
            src_ref=ysend, dst_ref=ybuf.at[f], send_sem=ys_sem.at[i], recv_sem=yr_sem.at[i],
            device_id=(g, s, ff), device_id_type=pl.DeviceIdType.MESH,
        )

    for i in (4, 3, 5, 2, 6, 1, 7):
        y_copy(i).start()

    def y_arrived(i):
        ff = lax.rem(f + 8 - i, 8)
        return pltpu.make_async_remote_copy(
            src_ref=ysend, dst_ref=ybuf.at[ff], send_sem=ys_sem.at[i], recv_sem=yr_sem.at[i],
            device_id=(g, s, ff), device_id_type=pl.DeviceIdType.MESH,
        )

    for i in range(1, 8):
        y_arrived(i).wait_recv()
    for n in range(8):
        dens[n * 10 : n * 10 + 10, :] = ybuf[n, 0:10, :].astype(f32)
    gat[z, x, core] = dens[...].astype(bf16)

    def at(n):
        if n == 0:
            return z
        return jnp.where(z > n - 1, n - 1, n)

    def z_copy(i, zz):
        return pltpu.make_async_remote_copy(
            src_ref=gat.at[z, x, core], dst_ref=gat.at[z, x, core], send_sem=zs_sem.at[i], recv_sem=zr_sem.at[i],
            device_id=z_dev(zz), device_id_type=pl.DeviceIdType.MESH,
        )

    def z_arrived(n):
        i = lax.rem(z + 8 - at(n), 8)
        return pltpu.make_async_remote_copy(
            src_ref=gat.at[z, x, core], dst_ref=gat.at[at(n), x, core], send_sem=zs_sem.at[i], recv_sem=zr_sem.at[i],
            device_id=z_dev(at(n)), device_id_type=pl.DeviceIdType.MESH,
        )

    def x_copy(n, d):
        piece = gat.at[at(n), x, core]
        return pltpu.make_async_remote_copy(
            src_ref=piece, dst_ref=piece, send_sem=xs_sem.at[n, d], recv_sem=xr_sem.at[at(n), d],
            device_id=x_dev(lax.rem(x + d, 4)), device_id_type=pl.DeviceIdType.MESH,
        )

    def x_arrived(n, d):
        xx = lax.rem(x + 4 - d, 4)
        piece = gat.at[at(n), xx, core]
        return pltpu.make_async_remote_copy(
            src_ref=piece, dst_ref=piece, send_sem=xs_sem.at[n, d], recv_sem=xr_sem.at[at(n), d],
            device_id=x_dev(xx), device_id_type=pl.DeviceIdType.MESH,
        )

    def c_copy(n, d, cc):
        xx = lax.rem(x + d, 4)
        piece = gat.at[at(n), xx, cc]
        return pltpu.make_async_remote_copy(
            src_ref=piece, dst_ref=piece, send_sem=cs_sem.at[n, d], recv_sem=cr_sem.at[n, d],
            device_id=partner, device_id_type=pl.DeviceIdType.MESH,
        )

    def spread(n):
        if n > 0:
            z_arrived(n).wait_recv()
        for d in (2, 1, 3):
            x_copy(n, d).start()
        c_copy(n, 0, core).start()

    def share(n):
        for d in (1, 3, 2):
            x_arrived(n, d).wait_recv()
            c_copy(n, 4 - d, core).start()

    def complete(n):
        for d in range(4):
            c_copy(n, d, 1 - core).wait_recv()

    def keys(*pieces):
        rows = jnp.concatenate([gat[at(n)].reshape(640, 128) for n in pieces], axis=0)
        size = 640 * len(pieces)
        wide = size // 128
        p2 = jnp.concatenate([rows, rows], axis=1)
        out = nt_dot(wkv[256:768, :], p2)
        pt = out[384:512]
        y = (out[256:384] + jnp.concatenate([gcol[...]] * wide, axis=1)) * pt
        row16 = lax.broadcasted_iota(jnp.int32, (16, size), 0)
        for half in range(2):
            ms = jnp.sum(y[half * 64 : half * 64 + 64], axis=0, keepdims=True) + bb
            inv = lax.rsqrt(jnp.maximum(ms, 0.0) * (1.0 / D) + EPS)
            kr = out[half * 128 : half * 128 + 128]
            kr = (kr + jnp.concatenate([bias_k[0]] * wide, axis=1)) * inv + jnp.concatenate([bias_k[1]] * wide, axis=1)
            ks = lax.rsqrt(jnp.sum(kr * kr, axis=0, keepdims=True) * (1.0 / 128) + EPS)
            first = pieces[0] * 1280 + half * size
            cols = slice(first, first + size)
            kt[:, cols] = (kr * ks).astype(bf16)
            vt[0:64, cols] = (pt[half * 64 : half * 64 + 64] * inv).astype(bf16)
            inv_hi = inv.astype(bf16).astype(f32)
            extra = jnp.where(row16 == 0, inv_hi, jnp.where(row16 == 1, 1.0, jnp.where(row16 == 2, inv - inv_hi, 0.0)))
            vt[64:80, cols] = extra.astype(bf16)

    def attend(half, *pieces):
        rows = slice(half * 160, half * 160 + 160)
        cols = slice(pieces[0] * 1280, pieces[-1] * 1280 + 1280)
        w = jnp.exp2(jnp.dot(q[rows], kt[:, cols], preferred_element_type=f32))
        acc[rows] += nt_dot(w.astype(bf16), vt[:, cols])

    for i in (1, 7, 2, 6, 3, 5, 4):
        z_copy(i, lax.rem(z + i, 8)).start()
    spread(0)
    for n in range(1, 8):
        spread(n)
    share(0)
    share(1)
    share(2)
    complete(0)
    keys(0)
    share(3)
    complete(1)
    keys(1)
    share(4)
    complete(2)
    keys(2)
    share(5)
    complete(3)
    keys(3)
    share(6)
    complete(4)
    keys(4)
    share(7)
    complete(5)
    complete(6)
    keys(5, 6)
    complete(7)
    fq, gq, hq = s // 4, z % 2, core
    pick_row = lax.broadcasted_iota(jnp.int32, (16, 80), 0)
    pick_col = lax.broadcasted_iota(jnp.int32, (16, 80), 1)
    pick = jnp.where((pick_row < 10) & (pick_col == pick_row + fq * 10), 1.0, 0.0).astype(bf16)
    for hx in range(2):
        blocks = [gat[zz, hx * 2 + gq, cc] for zz in range(8) for cc in range(2)]
        picked = jnp.dot(pick, jnp.concatenate(blocks, axis=1), preferred_element_type=f32)
        for n in range(16):
            qscr[hx * 16 + n] = picked[:, n * 128 : (n + 1) * 128]
    qall = qscr[...]
    for i in range(10):
        qrows[i * 32 : (i + 1) * 32, :] = qall[:, i, :]
    qp = qrows[...]
    qb = qp.astype(bf16)
    q2 = jnp.concatenate([qb, qb], axis=1)
    wq = jnp.where(hq == 0, wkv[0:128, :].astype(f32), wkv[128:256, :].astype(f32)).astype(bf16)
    raw = nt_dot(q2, wq)
    gp = nt_dot(q2, wkv[512:640, :])
    lane320 = lax.broadcasted_iota(jnp.int32, (320, 128), 1)
    y = jnp.where(lane320 // 64 == hq, (gp + grow2) * qp, 0.0)
    ms = jnp.sum(y, axis=1, keepdims=True) + bb
    inv = lax.rsqrt(jnp.maximum(ms, 0.0) * (1.0 / D) + EPS)
    c_q = res[128:129, 0:128] + res[136:137, 0:128]
    d_q = res[129:130, 0:128] + res[137:138, 0:128]
    qr = (raw + c_q) * inv + d_q
    qs = lax.rsqrt(jnp.sum(qr * qr, axis=1, keepdims=True) * (1.0 / 128) + EPS)
    q = (qr * qs * (qg_ref[...] * kg_ref[...] * (math.log2(math.e) / math.sqrt(128.0)))).astype(bf16)
    def a_copy(i, src, slot, j):
        return pltpu.make_async_remote_copy(
            src_ref=asend.at[src], dst_ref=arecv.at[slot], send_sem=as_sem.at[i], recv_sem=ar_sem.at[i],
            device_id=(j // 8, s, j % 8), device_id_type=pl.DeviceIdType.MESH,
        )

    pad = jnp.zeros((12, 128), f32)

    def finish(half):
        u = acc[half * 160 : half * 160 + 160]
        hi, lo = hi_lo(u)
        numer = jnp.dot(jnp.concatenate([hi, lo, hi], axis=1), wv[...], preferred_element_type=f32)
        out = numer / u[:, 65:66]
        for n in range(8):
            piece = jnp.concatenate([out[n * 20 : n * 20 + 20], pad], axis=0)
            asend[half * 8 + n] = piece.astype(bf16)

        for k in (4, 3, 5, 2, 6, 1, 7, 0):
            j = half * 8 + lax.rem(f + k, 8)

            @pl.when(j != head)
            def _():
                a_copy(lax.rem(j - head + 16, 16), j, head, j).start()

    attend(0, 0, 1)
    attend(0, 2, 3)
    keys(7)
    attend(0, 4, 5)
    attend(0, 6, 7)
    finish(0)
    for first in (0, 2, 4, 6):
        attend(1, first, first + 1)
    finish(1)
    arecv[head] = asend[head]

    for a, t in halo:
        halo_copy(a, t).wait_send()
    for i in range(1, 8):
        y_copy(i).wait_send()
        z_copy(i, lax.rem(z + i, 8)).wait_send()
    for n in range(8):
        for d in range(1, 4):
            x_copy(n, d).wait_send()
        for d in range(4):
            c_copy(n, d, core).wait_send()

    def head_arrived(i, _):
        j = lax.rem(head + 16 - i, 16)
        a_copy(i, j, j, j).wait_recv()
        return 0

    lax.fori_loop(1, 16, head_arrived, 0)

    def head_sent(i, _):
        j = lax.rem(head + i, 16)
        a_copy(i, j, head, j).wait_send()
        return 0

    lax.fori_loop(1, 16, head_sent, 0)


def local(
    enc_features, conv_weight, conv_bias, embed_weight, embed_bias, mod_shift, mod_scale, qkv_weight, q_gain, k_gain
):
    vmem = pl.BlockSpec(memory_space=pltpu.VMEM)
    hbm = pl.BlockSpec(memory_space=pltpu.HBM)
    dma = pltpu.SemaphoreType.DMA
    out = pl.pallas_call(
        kernel,
        out_shape=jax.ShapeDtypeStruct((16, 32, 128), bf16),
        in_specs=[hbm] * 10,
        out_specs=vmem,
        scratch_shapes=[
            pltpu.VMEM((80, 2, 512), bf16),
            pltpu.VMEM((432, 512), bf16),
            pltpu.VMEM((1, 16), f32),
            pltpu.VMEM((64, D), bf16),
            pltpu.VMEM((1, D), f32),
            pltpu.VMEM((1, D), f32),
            pltpu.VMEM((1, D), f32),
            pltpu.VMEM((3, D, 128), bf16),
            pltpu.VMEM((1, 128), f32),
            pltpu.VMEM((1, 128), f32),
            pltpu.VMEM((3, 24, 128), f32),
            pltpu.VMEM((3, 3, 24, 128), f32),
            pltpu.VMEM((8, 16, 128), bf16),
            pltpu.VMEM((16, 128), bf16),
            pltpu.VMEM((80, 128), f32),
            pltpu.VMEM((8, 4, 2, 80, 128), bf16),
            pltpu.VMEM((144, 384), f32),
            pltpu.VMEM((128, 128), f32),
            pltpu.VMEM((768, 256), bf16),
            pltpu.VMEM((384, 128), bf16),
            pltpu.VMEM((2, 128, 128), f32),
            pltpu.VMEM((128, 128), f32),
            pltpu.VMEM((128, 10240), bf16),
            pltpu.VMEM((128, 10240), bf16),
            pltpu.VMEM((32, 16, 128), f32),
            pltpu.VMEM((320, 128), f32),
            pltpu.VMEM((320, 128), f32),
            pltpu.VMEM((16, 32, 128), bf16),
            dma((10,)),
            dma((9,)),
            dma((9,)),
            dma((8,)),
            dma((8,)),
            dma((8,)),
            dma((8,)),
            dma((8, 4)),
            dma((8, 4)),
            dma((8, 4)),
            dma((8, 4)),
            dma((16,)),
            dma((16,)),
        ],
        compiler_params=pltpu.CompilerParams(
            collective_id=0, has_side_effects=True, vmem_limit_bytes=60 * 1024 * 1024
        ),
        cost_estimate=pl.CostEstimate(flops=5_000_000_000, bytes_accessed=6_000_000, transcendentals=3_300_000),
    )(
        enc_features.reshape(80, 2, 512),
        conv_weight.transpose(0, 1, 2, 4, 3).reshape(432, 512),
        conv_bias.reshape(1, 16),
        embed_weight,
        embed_bias.reshape(1, D),
        mod_shift.reshape(1, D),
        mod_scale.reshape(1, D),
        qkv_weight.transpose(1, 2, 0, 3).reshape(3, D, 128),
        q_gain.reshape(1, 128),
        k_gain.reshape(1, 128),
    )
    return out[:, :20, :].transpose(1, 0, 2).reshape(1, 1, 20, 2048)


def solution(mesh):
    in_specs = (
        P("tile", None, "seq", None), P(), P(), P(), P(), P(), P(), P(None, None, ("grp", "tile"), None), P(), P(),
    )
    out_specs = P("seq", ("grp", "tile"), None, None)
    return jax.shard_map(local, mesh=mesh, in_specs=in_specs, out_specs=out_specs, check_vma=False)
```
